128 devices in a mesh: dp: 4 (over y_lo, core), ctx: 32 (over y_hi, x, z).
Axes of the slice: x: 4, y: 4 (y_hi: 2, y_lo: 2; y = y_hi * 2 + y_lo), z: 4, core: 2. Of those that a mesh axis runs over, the one named last changes fastest.
Arguments:
- hidden: bfloat16 [4, 8192, 4096], P('dp', 'ctx'), may hold values from -6 to 6
- projected: bfloat16 [3, 4, 8192, 2048], P(None, 'dp', 'ctx'), may hold values from -72 to 72, as said below
- output_gradient: bfloat16 [4, 8192, 4096], P('dp', 'ctx'), may hold values from -6 to 6
- output_weight: bfloat16 [2048, 4096], replicated, may hold values from -0.125 to 0.125
- adapter_down_weight: bfloat16 [3, 8, 4096], replicated, may hold values from -0.09375 to 0.09375
- adapter_up_weight: bfloat16 [3, 8, 2048], replicated, may hold values from -2 to 2
- output_down_weight: bfloat16 [8, 2048], replicated, may hold values from -0.125 to 0.125
- output_up_weight: bfloat16 [8, 4096], replicated, may hold values from -2 to 2
Outputs:
- input_gradient: bfloat16 [4, 8192, 4096], P('dp', 'ctx')
- grad_down: bfloat16 [3, 8, 4096], replicated
- grad_up: bfloat16 [3, 8, 2048], replicated
- grad_down_o: bfloat16 [8, 2048], replicated
- grad_up_o: bfloat16 [8, 4096], replicated
The draws below stay inside these ranges and needn't reach their ends.
Inputs may be any that keep to these rules, and one draw needn't show every extreme that they name: `projected`: queries, keys and values, heads side by side along the last dimension.
All inputs are finite; a program needn't handle non-finite values.
Results may differ from the reference program's by a relative error of at most 0.0085.
Values may be sent and summed in bfloat16 or wider, within the bound.
A program may use at most 128 MiB of HBM per device.

```python
import math
import jax
import jax.numpy as jnp
from jax import lax

MODEL_WIDTH = 4096
HEAD_WIDTH = 128
HALF_HEADS = 16
ADAPTER_RANK = 8
GROUP = 512
SHIFT = 256
SEQUENCE_LENGTH = 8192
SEQUENCE_COUNT = 4


def draw_projected(key, part):
    key = jax.random.fold_in(key, 17)
    subkeys = jax.random.split(key, 1)
    full_width = HALF_HEADS * HEAD_WIDTH
    drawn = jnp.clip(jax.random.normal(subkeys[0], (3, SEQUENCE_COUNT, SEQUENCE_LENGTH, full_width), jnp.float32), -6.0, 6.0)
    return drawn.astype(jnp.bfloat16)


def steps_of(key, shape, pieces, low, top_value):
    gain = 1.0
    for axis_at, shards_of in pieces:
        draws = jax.random.uniform(jax.random.fold_in(jax.random.fold_in(key, 6), axis_at), (shards_of,), jnp.float32, low / len(pieces), top_value / len(pieces))
        gain = gain * jnp.repeat(jnp.exp(draws), shape[axis_at] // shards_of).reshape((-1,) + (1,) * (len(shape) - 1 - axis_at))
    return gain


def centred(key, shape, width, reach, shards=(), dtype=jnp.bfloat16):
    entries = jax.random.normal(key, shape, jnp.float32) * width
    if len(shards) > 0:
        entries = steps_of(key, shape, shards, -0.22, 0.18) * entries
    return jnp.clip(entries, min=-reach, max=reach).astype(dtype)


def setup_inputs(seed: int = 0) -> dict:
    splits = jax.random.split(jax.random.key(seed), 9)
    return {
        "hidden": centred(splits[0], (SEQUENCE_COUNT, SEQUENCE_LENGTH, MODEL_WIDTH), 1.0, 6.0, ((0, 4), (1, 32))),
        "projected": draw_projected(jax.random.fold_in(splits[8], 71), 0),
        "output_gradient": centred(splits[2], (SEQUENCE_COUNT, SEQUENCE_LENGTH, MODEL_WIDTH), 1.0, 6.0, ((0, 4), (1, 32))),
        "output_weight": centred(splits[3], (HALF_HEADS * HEAD_WIDTH, MODEL_WIDTH), (HALF_HEADS * HEAD_WIDTH) ** -0.5, 0.125),
        "adapter_down_weight": centred(splits[4], (3, ADAPTER_RANK, MODEL_WIDTH), MODEL_WIDTH ** -0.5, 0.09375),
        "adapter_up_weight": centred(splits[5], (3, ADAPTER_RANK, HALF_HEADS * HEAD_WIDTH), ADAPTER_RANK ** -0.5, 2.0),
        "output_down_weight": centred(splits[6], (ADAPTER_RANK, HALF_HEADS * HEAD_WIDTH), (HALF_HEADS * HEAD_WIDTH) ** -0.5, 0.125),
        "output_up_weight": centred(splits[7], (ADAPTER_RANK, MODEL_WIDTH), ADAPTER_RANK ** -0.5, 2.0),
    }


ADAPTER_SCALE = 2.0

def rounded(tensor):
    return lax.optimization_barrier(tensor.astype(jnp.bfloat16)).astype(jnp.float32)

def group_attention(queries, key_rows, values, attention_gradient):
    score_scale = 1.0 / math.sqrt(HEAD_WIDTH)
    length = queries.shape[1]
    half_rows = length // 2
    key_full = key_rows.astype(jnp.float32)
    value_full = values.astype(jnp.float32)
    query_full = queries.astype(jnp.float32)
    d_full = attention_gradient.astype(jnp.float32)
    scores = jnp.einsum('gqhe,gkhe->ghqk', query_full, key_full) * score_scale
    position = jnp.arange(length)
    causal = position[:, None] >= position[None, :]
    scores = jnp.where(causal, scores, -jnp.inf)
    row_max = lax.optimization_barrier(jnp.max(scores, axis=-1, keepdims=True))
    raised = jnp.exp(scores - row_max)
    attn_probs = raised / lax.optimization_barrier(jnp.sum(raised, axis=-1, keepdims=True))
    probs_low = rounded(attn_probs)
    attended = jnp.einsum('ghqk,gkhe->gqhe', probs_low, value_full).astype(jnp.bfloat16)
    d_probs = jnp.einsum('gqhe,gkhe->ghqk', d_full, value_full)
    row_dot = lax.optimization_barrier(jnp.sum(attn_probs * d_probs, axis=-1, keepdims=True))
    d_scores = rounded(attn_probs * (d_probs - row_dot))
    query_gradient = jnp.einsum('ghqk,gkhe->gqhe', d_scores, key_full) * score_scale
    near_keys = jnp.einsum('ghqk,gqhe->gkhe', d_scores[:, :, :half_rows], query_full[:, :half_rows]) * score_scale
    far_keys = jnp.einsum('ghqk,gqhe->gkhe', d_scores[:, :, half_rows:], query_full[:, half_rows:]) * score_scale
    key_gradient = near_keys + rounded(far_keys)
    near_values = jnp.einsum('ghqk,gqhe->gkhe', probs_low[:, :, :half_rows], d_full[:, :half_rows])
    far_values = jnp.einsum('ghqk,gqhe->gkhe', probs_low[:, :, half_rows:], d_full[:, half_rows:])
    value_gradient = near_values + rounded(far_values)
    return (attended, query_gradient.astype(jnp.bfloat16), key_gradient.astype(jnp.bfloat16), value_gradient.astype(jnp.bfloat16))

def regroup(matrix, offset):
    return jnp.roll(matrix, -offset, axis=0).reshape(SEQUENCE_LENGTH // GROUP, GROUP, HALF_HEADS // 2, HEAD_WIDTH)

def ungroup(tensor, offset):
    return jnp.roll(tensor.reshape(SEQUENCE_LENGTH, -1), offset, axis=0)

def head_set(queries, key_rows, values, attention_gradient, offset):
    outputs = group_attention(regroup(queries, offset), regroup(key_rows, offset), regroup(values, offset), regroup(attention_gradient, offset))
    return tuple((ungroup(output, offset) for output in outputs))

def reference(hidden, projected, output_gradient, output_weight, adapter_down_weight, adapter_up_weight, output_down_weight, output_up_weight):
    half_width = HALF_HEADS * HEAD_WIDTH // 2

    def one_sequence(inputs):
        hidden_token_rows, proj_rows, gradient_rows = inputs
        output_thin_gradient = jnp.dot(gradient_rows, output_up_weight.T, preferred_element_type=jnp.float32).astype(jnp.bfloat16)
        attention_gradient = (jnp.dot(gradient_rows, output_weight.T, preferred_element_type=jnp.float32) + ADAPTER_SCALE * jnp.dot(output_thin_gradient, output_down_weight, preferred_element_type=jnp.float32)).astype(jnp.bfloat16)
        unshifted = head_set(proj_rows[0, :, :half_width], proj_rows[1, :, :half_width], proj_rows[2, :, :half_width], attention_gradient[:, :half_width], 0)
        shifted = head_set(proj_rows[0, :, half_width:], proj_rows[1, :, half_width:], proj_rows[2, :, half_width:], attention_gradient[:, half_width:], SHIFT)
        attended = jnp.concatenate([unshifted[0], shifted[0]], axis=1)
        query_key_value_gradient = jnp.stack([jnp.concatenate([unshifted[1], shifted[1]], axis=1), jnp.concatenate([unshifted[2], shifted[2]], axis=1), jnp.concatenate([unshifted[3], shifted[3]], axis=1)])
        low_o = jnp.dot(attended, output_down_weight.T, preferred_element_type=jnp.float32).astype(jnp.bfloat16)
        part_up_o = jnp.dot(low_o.T, gradient_rows, preferred_element_type=jnp.float32)
        part_down_o = jnp.dot(output_thin_gradient.T, attended, preferred_element_type=jnp.float32)
        ups = []
        downs = []
        inner_total_sum = jnp.zeros((SEQUENCE_LENGTH, MODEL_WIDTH), jnp.float32)
        for projection_member in range(3):
            thin_input = jnp.dot(hidden_token_rows, adapter_down_weight[projection_member].T, preferred_element_type=jnp.float32).astype(jnp.bfloat16)
            thin_gradient = jnp.dot(query_key_value_gradient[projection_member], adapter_up_weight[projection_member].T, preferred_element_type=jnp.float32).astype(jnp.bfloat16)
            ups.append(jnp.dot(thin_input.T, query_key_value_gradient[projection_member], preferred_element_type=jnp.float32))
            downs.append(jnp.dot(thin_gradient.T, hidden_token_rows, preferred_element_type=jnp.float32))
            inner_total_sum = inner_total_sum + jnp.dot(thin_gradient, adapter_down_weight[projection_member], preferred_element_type=jnp.float32)
        input_gradient = (ADAPTER_SCALE * inner_total_sum).astype(jnp.bfloat16)
        return (input_gradient, jnp.stack(downs), jnp.stack(ups), part_down_o, part_up_o)
    results = lax.map(one_sequence, (hidden, jnp.swapaxes(projected, 0, 1), output_gradient))
    scale_factor = ADAPTER_SCALE / (SEQUENCE_COUNT * SEQUENCE_LENGTH)
    return (results[0], (scale_factor * lax.optimization_barrier(jnp.sum(results[1], axis=0))).astype(jnp.bfloat16), (scale_factor * lax.optimization_barrier(jnp.sum(results[2], axis=0))).astype(jnp.bfloat16), (scale_factor * lax.optimization_barrier(jnp.sum(results[3], axis=0))).astype(jnp.bfloat16), (scale_factor * lax.optimization_barrier(jnp.sum(results[4], axis=0))).astype(jnp.bfloat16))
```

```python
import functools
import math

import jax
import jax.numpy as jnp
from jax import lax
from jax.experimental import pallas as pl
from jax.experimental.pallas import tpu as pltpu
from jax.sharding import PartitionSpec as P

MESH = pl.DeviceIdType.MESH
DMA = pltpu.SemaphoreType.DMA
VMEM = pltpu.VMEM
F32 = jnp.float32
BF16 = jnp.bfloat16

TOKENS = 256
MODEL = 4096
HEADS_WIDTH = 2048
HALF = 1024
HEAD = 128
RANK = 8
CTX = 32
SCALE = 1.0 / math.sqrt(HEAD)
EXP2_SCALE = SCALE * math.log2(math.e)
GRAD_SCALE = 2.0 / 32768
OW_BLOCK = 512

DOWN_AT = 0
UP_O_AT = 3 * MODEL
UP_AT = 4 * MODEL
DOWN_O_AT = 4 * MODEL + 3 * HEADS_WIDTH
PACKED = 4 * MODEL + 4 * HEADS_WIDTH
PACKED_HALF = PACKED // 2
CORE_LANES = PACKED // 4
PLANE = 16
CHUNK = CORE_LANES // PLANE


def nn(a, b):
    return lax.dot_general(a, b, (((1,), (0,)), ((), ())), preferred_element_type=F32)


def nt(a, b):
    return lax.dot_general(a, b, (((1,), (1,)), ((), ())), preferred_element_type=F32)


def tn(a, b):
    return lax.dot_general(a, b, (((0,), (0,)), ((), ())), preferred_element_type=F32)


def lanes(start, size):
    return pl.ds(pl.multiple_of(start, 128), size)


def attention_kernel(
    hidden_hbm,
    projected_hbm,
    gradient_hbm,
    weight_hbm,
    down_ref,
    up_ref,
    down_o_ref,
    up_o_ref,
    d_low_ref,
    packed_ref,
    hid,
    q,
    k,
    v,
    og,
    ow,
    far_k,
    far_v,
    d_attn,
    att,
    dq,
    dk,
    dv,
    dk_far,
    dv_far,
    low_own,
    low_far,
    d_low_send,
    d_low_recv,
    in_sem,
    ow_sem,
    qkv_sem,
    kv_send_sem,
    kv_recv_sem,
    small_send_sem,
    small_recv_sem,
):
    dp = lax.axis_index("dp")
    ctx = lax.axis_index("ctx")
    following = (dp, lax.rem(ctx + 1, CTX))
    previous = (dp, lax.rem(ctx + CTX - 1, CTX))
    parity = lax.rem(ctx, 2)
    first_start = parity * HALF
    pair_start = (1 - parity) * HALF

    barrier = pltpu.get_barrier_semaphore()
    pl.semaphore_signal(barrier, inc=1, device_id=following, device_id_type=MESH)
    pl.semaphore_signal(barrier, inc=1, device_id=previous, device_id_type=MESH)

    def ow_copy(block):
        half = block // (HALF // OW_BLOCK)
        start = jnp.where(half == 0, first_start, pair_start)
        row = start + lax.rem(block, HALF // OW_BLOCK) * OW_BLOCK
        return pltpu.make_async_copy(
            weight_hbm.at[pl.ds(pl.multiple_of(row, OW_BLOCK), OW_BLOCK), :],
            ow.at[pl.ds(pl.multiple_of(block * OW_BLOCK, OW_BLOCK), OW_BLOCK), :],
            ow_sem.at[block],
        )

    og_copy = pltpu.make_async_copy(gradient_hbm.at[0], og, in_sem.at[0])
    hid_copy = pltpu.make_async_copy(hidden_hbm.at[0], hid, in_sem.at[1])
    qkv_copies = [
        [
            pltpu.make_async_copy(
                projected_hbm.at[c, 0, :, lanes(start, HALF)],
                ref.at[:, at * HALF : (at + 1) * HALF],
                qkv_sem.at[at, c],
            )
            for c, ref in enumerate((q, k, v))
        ]
        for at, start in enumerate((first_start, pair_start))
    ]
    og_copy.start()
    hid_copy.start()
    ow_copy(0).start()
    ow_copy(1).start()
    for copy in qkv_copies[0]:
        copy.start()
    ow_copy(2).start()
    ow_copy(3).start()
    for copy in qkv_copies[1]:
        copy.start()

    pl.semaphore_wait(barrier, 2)
    kv_copies = []
    for j in range(4):
        for c, ref in ((0, far_k), (1, far_v)):
            copy = pltpu.make_async_remote_copy(
                src_ref=projected_hbm.at[c + 1, 0, :, lanes(first_start + j * 256, 256)],
                dst_ref=ref.at[:, j * 256 : (j + 1) * 256],
                send_sem=kv_send_sem.at[j, c],
                recv_sem=kv_recv_sem.at[j, c],
                device_id=following,
                device_id_type=MESH,
            )
            copy.start()
            kv_copies.append(copy)

    og_copy.wait()
    dy_low = nt(up_o_ref[...], og[...]).astype(BF16)
    hid_copy.wait()
    low_in = nt(down_ref[...], hid[...]).astype(BF16)
    low_own[...] = low_in[RANK:]
    low_copy = pltpu.make_async_remote_copy(
        src_ref=low_own,
        dst_ref=low_far,
        send_sem=small_send_sem.at[0],
        recv_sem=small_recv_sem.at[0],
        device_id=following,
        device_id_type=MESH,
    )
    low_copy.start()

    def project(block, carry):
        ow_copy(block).wait()
        half = block // (HALF // OW_BLOCK)
        start = jnp.where(half == 0, first_start, pair_start)
        column = start + lax.rem(block, HALF // OW_BLOCK) * OW_BLOCK
        rows = pl.ds(pl.multiple_of(block * OW_BLOCK, OW_BLOCK), OW_BLOCK)
        through_adapter = tn(down_o_ref[:, lanes(column, OW_BLOCK)], dy_low)
        d_attn[rows, :] = (nt(ow[rows, :], og[...]) + 2.0 * through_adapter).astype(BF16)
        return carry

    lax.fori_loop(0, HEADS_WIDTH // OW_BLOCK, project, 0)

    key_row = lax.broadcasted_iota(jnp.int32, (TOKENS, TOKENS), 0)
    query_column = lax.broadcasted_iota(jnp.int32, (TOKENS, TOKENS), 1)
    seen = key_row <= query_column

    def head(at, far_at):
        cols = lanes(at, HEAD)
        rows = pl.ds(pl.multiple_of(at, HEAD), HEAD)
        q_head = q[:, cols]
        d_head = d_attn[rows, :]
        keys = [k[:, cols]]
        values = [v[:, cols]]
        if far_at is not None:
            far_cols = lanes(far_at, HEAD)
            keys.append(far_k[:, far_cols])
            values.append(far_v[:, far_cols])
        scores = [nt(key, q_head) * EXP2_SCALE for key in keys]
        scores[0] = jnp.where(seen, scores[0], -jnp.inf)
        row_max = functools.reduce(
            jnp.maximum, [jnp.max(score, axis=0, keepdims=True) for score in scores]
        )
        raised = [jnp.exp2(score - row_max) for score in scores]
        total = sum(jnp.sum(r, axis=0, keepdims=True) for r in raised)
        inverse = 1.0 / total
        probs = [r * inverse for r in raised]
        probs_low = [p.astype(BF16) for p in probs]
        d_probs = [nn(value, d_head) for value in values]
        row_dot = sum(
            jnp.sum(p * d, axis=0, keepdims=True) for p, d in zip(probs, d_probs)
        )
        d_scores = [(p * (d - row_dot)).astype(BF16) for p, d in zip(probs, d_probs)]
        att[rows, :] = sum(tn(value, p) for value, p in zip(values, probs_low)).astype(BF16)
        dq[rows, :] = (sum(tn(key, s) for key, s in zip(keys, d_scores)) * SCALE).astype(BF16)
        dk[:, cols] = (nn(d_scores[0], q_head) * SCALE).astype(BF16)
        dv[:, cols] = nt(probs_low[0], d_head).astype(BF16)
        if far_at is not None:
            dk_far[:, far_cols] = (nn(d_scores[1], q_head) * SCALE).astype(BF16)
            dv_far[:, far_cols] = nt(probs_low[1], d_head).astype(BF16)

    for copy in qkv_copies[0]:
        copy.wait()

    def first_heads(j, carry):
        for i in range(2):
            head(j * 256 + i * HEAD, None)
        return carry

    lax.fori_loop(0, 4, first_heads, 0)
    for copy in qkv_copies[1]:
        copy.wait()

    def pair_heads(j, carry):
        for c, ref in ((0, far_k), (1, far_v)):
            part = ref.at[:, lanes(j * 256, 256)]
            pltpu.make_async_copy(part, part, kv_recv_sem.at[j, c]).wait()
        for i in range(2):
            head(HALF + j * 256 + i * HEAD, j * 256 + i * HEAD)
        return carry

    lax.fori_loop(0, 4, pair_heads, 0)

    halves = ((0, first_start), (HALF, pair_start))

    d_low_send[:RANK] = nt(up_ref[1, :, lanes(pair_start, HALF)], dk_far[...])
    d_low_send[RANK:] = nt(up_ref[2, :, lanes(pair_start, HALF)], dv_far[...])
    d_low_copy = pltpu.make_async_remote_copy(
        src_ref=d_low_send,
        dst_ref=d_low_recv,
        send_sem=small_send_sem.at[1],
        recv_sem=small_recv_sem.at[1],
        device_id=previous,
        device_id_type=MESH,
    )
    d_low_copy.start()

    low_o = sum(
        nn(down_o_ref[:, lanes(start, HALF)], att[at : at + HALF, :]) for at, start in halves
    ).astype(BF16)
    packed_ref[:, UP_O_AT : UP_O_AT + MODEL] = nn(low_o, og[...])
    for at, start in halves:
        packed_ref[:, lanes(DOWN_O_AT + start, HALF)] = nt(dy_low, att[at : at + HALF, :])
        packed_ref[:, lanes(UP_AT + start, HALF)] = nt(low_in[:RANK], dq[at : at + HALF, :])
    low_copy.wait()
    for c, near, far in ((1, dk, dk_far), (2, dv, dv_far)):
        own = low_in[c * RANK : (c + 1) * RANK]
        at_c = UP_AT + c * HEADS_WIDTH
        packed_ref[:, lanes(at_c + first_start, HALF)] = nn(own, near[:, :HALF])
        packed_ref[:, lanes(at_c + pair_start, HALF)] = nn(own, near[:, HALF:]) + nn(
            low_far[(c - 1) * RANK : c * RANK], far[...]
        )
    d_low = [
        sum(nn(up_ref[0, :, lanes(start, HALF)], dq[at : at + HALF, :]) for at, start in halves)
    ]
    for c, near in ((1, dk), (2, dv)):
        d_low.append(
            sum(
                nt(up_ref[c, :, lanes(start, HALF)], near[:, at : at + HALF])
                for at, start in halves
            )
        )
    d_low_copy.wait()
    d_low[1] += d_low_recv[:RANK]
    d_low[2] += d_low_recv[RANK:]
    d_low = jnp.concatenate(d_low, axis=0).astype(BF16)
    d_low_ref[...] = d_low
    down = nn(d_low, hid[...])
    for c in range(3):
        packed_ref[:, DOWN_AT + c * MODEL : DOWN_AT + (c + 1) * MODEL] = down[
            c * RANK : (c + 1) * RANK
        ]
    for copy in kv_copies:
        copy.wait_send()


def attention_part(hidden, projected, gradient, weight, down, up, down_o, up_o):
    half = VMEM((TOKENS, HALF), BF16)
    whole = VMEM((TOKENS, HEADS_WIDTH), BF16)
    flipped = VMEM((HEADS_WIDTH, TOKENS), BF16)
    wide = VMEM((TOKENS, MODEL), BF16)
    anywhere = pl.BlockSpec(memory_space=pl.ANY)
    resident = pl.BlockSpec(memory_space=VMEM)
    return pl.pallas_call(
        attention_kernel,
        out_shape=(
            jax.ShapeDtypeStruct((3 * RANK, TOKENS), BF16),
            jax.ShapeDtypeStruct((RANK, PACKED), F32),
        ),
        in_specs=[anywhere] * 4 + [resident] * 4,
        out_specs=(resident, resident),
        scratch_shapes=[
            wide,
            whole,
            whole,
            whole,
            wide,
            VMEM((HEADS_WIDTH, MODEL), BF16),
            half,
            half,
            flipped,
            flipped,
            flipped,
            whole,
            whole,
            half,
            half,
            VMEM((2 * RANK, TOKENS), BF16),
            VMEM((2 * RANK, TOKENS), BF16),
            VMEM((2 * RANK, TOKENS), F32),
            VMEM((2 * RANK, TOKENS), F32),
            DMA((2,)),
            DMA((4,)),
            DMA((2, 3)),
            DMA((4, 2)),
            DMA((4, 2)),
            DMA((2,)),
            DMA((2,)),
        ],
        compiler_params=pltpu.CompilerParams(
            collective_id=0, has_side_effects=True, vmem_limit_bytes=56 << 20
        ),
    )(hidden, projected, gradient, weight, down, up, down_o, up_o)


def reduce_kernel(
    part_ref,
    out_ref,
    pair_recv,
    low,
    plane_recv,
    mine,
    line_recv,
    pair_sems,
    plane_send,
    plane_recv_sem,
    line_send,
    line_recv_sem,
    back_send,
    back_recv_sem,
    last_sems,
):
    dp = lax.axis_index("dp")
    ctx = lax.axis_index("ctx")
    core = lax.rem(dp, 2)
    y_lo = dp // 2
    y_hi = ctx // PLANE
    place = lax.rem(ctx, PLANE)
    y = y_hi * 2 + y_lo

    def plane_peer(r):
        return (dp, y_hi * PLANE + lax.rem(place + r, PLANE))

    def line_peer(r):
        other_y = lax.rem(y + r, 4)
        return (lax.rem(other_y, 2) * 2 + core, (other_y // 2) * PLANE + place)

    other_core = (y_lo * 2 + 1 - core, ctx)
    barrier = pltpu.get_barrier_semaphore()
    pl.semaphore_signal(barrier, inc=1, device_id=other_core, device_id_type=MESH)
    for r in range(1, PLANE):
        pl.semaphore_signal(barrier, inc=1, device_id=plane_peer(r), device_id_type=MESH)
    for r in range(1, 4):
        pl.semaphore_signal(barrier, inc=1, device_id=line_peer(r), device_id_type=MESH)
    pl.semaphore_wait(barrier, PLANE + 3)

    pair_copies = []
    for row in range(2):
        copy = pltpu.make_async_remote_copy(
            src_ref=part_ref.at[
                :, lanes(row * PACKED_HALF + (1 - core) * CORE_LANES, CORE_LANES)
            ],
            dst_ref=pair_recv.at[row],
            send_sem=pair_sems.at[row, 0],
            recv_sem=pair_sems.at[row, 1],
            device_id=other_core,
            device_id_type=MESH,
        )
        copy.start()
        pair_copies.append(copy)
    for copy in pair_copies:
        copy.wait()
    for n in range(PLANE):
        rows = [
            part_ref[:, lanes(row * PACKED_HALF + core * CORE_LANES + n * CHUNK, CHUNK)]
            + pair_recv[row, :, n * CHUNK : (n + 1) * CHUNK]
            for row in range(2)
        ]
        low[n] = jnp.concatenate(rows, axis=0).astype(BF16)

    for r in range(1, PLANE):
        pltpu.make_async_remote_copy(
            src_ref=low.at[lax.rem(place + r, PLANE)],
            dst_ref=plane_recv.at[r - 1],
            send_sem=plane_send,
            recv_sem=plane_recv_sem,
            device_id=plane_peer(r),
            device_id_type=MESH,
        ).start()
    total = low[place].astype(F32)
    pltpu.make_async_copy(plane_recv, plane_recv, plane_recv_sem).wait()
    for r in range(PLANE - 1):
        total = total + plane_recv[r].astype(F32)
    mine[...] = total.astype(BF16)
    line_recv[y] = mine[...]
    for r in range(1, 4):
        pltpu.make_async_remote_copy(
            src_ref=mine,
            dst_ref=line_recv.at[y],
            send_sem=line_send,
            recv_sem=line_recv_sem,
            device_id=line_peer(r),
            device_id_type=MESH,
        ).start()
    three = line_recv.at[0:3]
    pltpu.make_async_copy(three, three, line_recv_sem).wait()
    total = line_recv[0].astype(F32)
    for r in range(1, 4):
        total = total + line_recv[r].astype(F32)
    out_ref[core, place] = (total * GRAD_SCALE).astype(BF16)
    for r in range(1, PLANE):
        pltpu.make_async_remote_copy(
            src_ref=out_ref.at[core, place],
            dst_ref=out_ref.at[core, place],
            send_sem=back_send,
            recv_sem=back_recv_sem,
            device_id=plane_peer(r),
            device_id_type=MESH,
        ).start()
    pltpu.make_async_copy(plane_recv, plane_recv, back_recv_sem).wait()
    last = pltpu.make_async_remote_copy(
        src_ref=out_ref.at[core],
        dst_ref=out_ref.at[core],
        send_sem=last_sems.at[0],
        recv_sem=last_sems.at[1],
        device_id=other_core,
        device_id_type=MESH,
    )
    last.start()
    pltpu.make_async_copy(plane_recv, plane_recv, plane_send).wait()
    pltpu.make_async_copy(three, three, line_send).wait()
    pltpu.make_async_copy(plane_recv, plane_recv, back_send).wait()
    last.wait()


def reduce_part(packed):
    resident = pl.BlockSpec(memory_space=VMEM)
    return pl.pallas_call(
        reduce_kernel,
        out_shape=jax.ShapeDtypeStruct((2, PLANE, 16, CHUNK), BF16),
        in_specs=[resident],
        out_specs=resident,
        scratch_shapes=[
            VMEM((2, RANK, CORE_LANES), F32),
            VMEM((PLANE, 16, CHUNK), BF16),
            VMEM((PLANE - 1, 16, CHUNK), BF16),
            VMEM((16, CHUNK), BF16),
            VMEM((4, 16, CHUNK), BF16),
            DMA((2, 2)),
            DMA,
            DMA,
            DMA,
            DMA,
            DMA,
            DMA,
            DMA((2,)),
        ],
        compiler_params=pltpu.CompilerParams(
            collective_id=1, has_side_effects=True, vmem_limit_bytes=32 << 20
        ),
    )(packed)


def finish_kernel(
    summed_ref, d_low_ref, down_ref, input_ref, grad_down_ref, grad_up_ref, down_o_ref, up_o_ref
):
    def place(tile, value):
        at = tile * 128
        if at < UP_O_AT:
            c, at = divmod(at, MODEL)
            grad_down_ref[c, :, at : at + 128] = value
        elif at < UP_AT:
            at -= UP_O_AT
            up_o_ref[:, at : at + 128] = value
        elif at < DOWN_O_AT:
            c, at = divmod(at - UP_AT, HEADS_WIDTH)
            grad_up_ref[c, :, at : at + 128] = value
        else:
            at -= DOWN_O_AT
            down_o_ref[:, at : at + 128] = value

    for core in range(2):
        for n in range(PLANE):
            for t in range(CHUNK // 128):
                block = summed_ref[core, n, :, t * 128 : (t + 1) * 128].astype(F32)
                tile = (core * CORE_LANES + n * CHUNK) // 128 + t
                for row in range(2):
                    place(
                        row * PACKED_HALF // 128 + tile,
                        block[row * RANK : (row + 1) * RANK].astype(BF16),
                    )
    for n in range(MODEL // 512):
        cols = slice(n * 512, (n + 1) * 512)
        input_ref[0, :, cols] = (2.0 * tn(d_low_ref[...], down_ref[:, cols])).astype(BF16)


def finish_part(summed, d_low, down):
    resident = pl.BlockSpec(memory_space=VMEM)
    return pl.pallas_call(
        finish_kernel,
        out_shape=(
            jax.ShapeDtypeStruct((1, TOKENS, MODEL), BF16),
            jax.ShapeDtypeStruct((3, RANK, MODEL), BF16),
            jax.ShapeDtypeStruct((3, RANK, HEADS_WIDTH), BF16),
            jax.ShapeDtypeStruct((RANK, HEADS_WIDTH), BF16),
            jax.ShapeDtypeStruct((RANK, MODEL), BF16),
        ),
        in_specs=[resident] * 3,
        out_specs=(resident,) * 5,
        compiler_params=pltpu.CompilerParams(vmem_limit_bytes=32 << 20),
    )(summed, d_low, down)


def per_device(hidden, projected, gradient, weight, down, up, down_o, up_o):
    down = down.reshape(3 * RANK, MODEL)
    d_low, packed = attention_part(hidden, projected, gradient, weight, down, up, down_o, up_o)
    summed = reduce_part(packed)
    return finish_part(summed, d_low, down)


def solution(mesh):
    in_specs = (
        P("dp", "ctx", None),
        P(None, "dp", "ctx", None),
        P("dp", "ctx", None),
        P(),
        P(),
        P(),
        P(),
        P(),
    )
    out_specs = (P("dp", "ctx", None), P(), P(), P(), P())
    return jax.shard_map(
        per_device, mesh=mesh, in_specs=in_specs, out_specs=out_specs, check_vma=False
    )
```

```python
import functools
import math

import jax
import jax.numpy as jnp
from jax import lax
from jax.experimental import pallas as pl
from jax.experimental.pallas import tpu as pltpu
from jax.sharding import PartitionSpec as P

MESH = pl.DeviceIdType.MESH
DMA = pltpu.SemaphoreType.DMA
VMEM = pltpu.VMEM
F32 = jnp.float32
BF16 = jnp.bfloat16

TOKENS = 256
MODEL = 4096
HEADS_WIDTH = 2048
HALF = 1024
HEAD = 128
RANK = 8
CTX = 32
SCALE = 1.0 / math.sqrt(HEAD)
EXP2_SCALE = SCALE * math.log2(math.e)
GRAD_SCALE = 2.0 / 32768
OW_BLOCK = 512

TILE = 128
LATE_SLOTS = 32
SLOTS = 48
DEVICES = 128


def nn(a, b):
    return lax.dot_general(a, b, (((1,), (0,)), ((), ())), preferred_element_type=F32)


def nt(a, b):
    return lax.dot_general(a, b, (((1,), (1,)), ((), ())), preferred_element_type=F32)


def tn(a, b):
    return lax.dot_general(a, b, (((0,), (0,)), ((), ())), preferred_element_type=F32)


def lanes(start, size):
    return pl.ds(pl.multiple_of(start, 128), size)


def stacked(top, bottom):
    return jnp.concatenate([top, bottom], axis=0).astype(BF16)


def tile_of(value, n):
    return value[:, n * TILE : (n + 1) * TILE]


def away(ctx, j, wide):
    x = lax.rem(ctx // 4 % 4 + 2 + j // 4 % 4, 4)
    z = lax.rem(ctx % 4 + 2 + j % 4, 4)
    if not wide:
        return x * 4 + z
    return lax.rem(ctx // 16 + 1 + j // 16 % 2, 2) * 16 + x * 4 + z


def attention_kernel(
    hidden_hbm,
    projected_hbm,
    gradient_hbm,
    weight_hbm,
    down_ref,
    up_ref,
    down_o_ref,
    up_o_ref,
    d_low_ref,
    summed_ref,
    hid,
    q,
    k,
    v,
    og,
    ow,
    far_k,
    far_v,
    d_attn,
    att,
    dq,
    dk,
    dv,
    dk_far,
    dv_far,
    low_own,
    low_far,
    d_low_send,
    d_low_recv,
    low,
    parts,
    in_sem,
    ow_sem,
    qkv_sem,
    kv_send_sem,
    kv_recv_sem,
    small_send_sem,
    small_recv_sem,
    part_send_sem,
    part_recv_sem,
    sum_send_sem,
    sum_recv_sem,
    last_sems,
):
    dp = lax.axis_index("dp")
    ctx = lax.axis_index("ctx")
    following = (dp, lax.rem(ctx + 1, CTX))
    previous = (dp, lax.rem(ctx + CTX - 1, CTX))
    parity = lax.rem(ctx, 2)
    first_start = parity * HALF
    pair_start = (1 - parity) * HALF

    core = lax.rem(dp, 2)
    y_lo = dp // 2
    me = dp * CTX + ctx

    barrier = pltpu.get_barrier_semaphore()

    def greet(n, carry):
        other = lax.rem(me + n, DEVICES)
        pl.semaphore_signal(
            barrier, inc=1, device_id=(other // CTX, lax.rem(other, CTX)), device_id_type=MESH
        )
        return carry

    def ow_copy(block):
        half = block // (HALF // OW_BLOCK)
        start = jnp.where(half == 0, first_start, pair_start)
        row = start + lax.rem(block, HALF // OW_BLOCK) * OW_BLOCK
        return pltpu.make_async_copy(
            weight_hbm.at[pl.ds(pl.multiple_of(row, OW_BLOCK), OW_BLOCK), :],
            ow.at[pl.ds(pl.multiple_of(block * OW_BLOCK, OW_BLOCK), OW_BLOCK), :],
            ow_sem.at[block],
        )

    og_copy = pltpu.make_async_copy(gradient_hbm.at[0], og, in_sem.at[0])
    hid_copy = pltpu.make_async_copy(hidden_hbm.at[0], hid, in_sem.at[1])
    qkv_copies = [
        [
            pltpu.make_async_copy(
                projected_hbm.at[c, 0, :, lanes(start, HALF)],
                ref.at[:, at * HALF : (at + 1) * HALF],
                qkv_sem.at[at, c],
            )
            for c, ref in enumerate((q, k, v))
        ]
        for at, start in enumerate((first_start, pair_start))
    ]
    og_copy.start()
    ow_copy(0).start()
    lax.fori_loop(1, DEVICES, greet, 0)
    pl.semaphore_wait(barrier, DEVICES - 1)
    kv_copies = []
    for j in range(4):
        for c, ref in ((0, far_k), (1, far_v)):
            copy = pltpu.make_async_remote_copy(
                src_ref=projected_hbm.at[c + 1, 0, :, lanes(first_start + j * 256, 256)],
                dst_ref=ref.at[:, j * 256 : (j + 1) * 256],
                send_sem=kv_send_sem.at[j, c],
                recv_sem=kv_recv_sem.at[j, c],
                device_id=following,
                device_id_type=MESH,
            )
            copy.start()
            kv_copies.append(copy)

    ow_copy(1).start()
    hid_copy.start()
    og_copy.wait()
    dy_low = nt(up_o_ref[...], og[...]).astype(BF16)

    def project(block, carry):
        ow_copy(block).wait()

        @pl.when(block < 2)
        def _():
            ow_copy(block + 2).start()

        half = block // (HALF // OW_BLOCK)
        start = jnp.where(half == 0, first_start, pair_start)
        column = start + lax.rem(block, HALF // OW_BLOCK) * OW_BLOCK
        rows = pl.ds(pl.multiple_of(block * OW_BLOCK, OW_BLOCK), OW_BLOCK)
        through_adapter = tn(down_o_ref[:, lanes(column, OW_BLOCK)], dy_low)
        d_attn[rows, :] = (nt(ow[rows, :], og[...]) + 2.0 * through_adapter).astype(BF16)
        return carry

    lax.fori_loop(0, 2, project, 0)
    for copies in qkv_copies:
        for copy in copies:
            copy.start()
    hid_copy.wait()
    low_in = nt(down_ref[...], hid[...]).astype(BF16)
    low_own[...] = low_in[RANK:]
    low_copy = pltpu.make_async_remote_copy(
        src_ref=low_own,
        dst_ref=low_far,
        send_sem=small_send_sem.at[0],
        recv_sem=small_recv_sem.at[0],
        device_id=following,
        device_id_type=MESH,
    )
    low_copy.start()
    lax.fori_loop(2, 4, project, 0)

    key_row = lax.broadcasted_iota(jnp.int32, (TOKENS, TOKENS), 0)
    query_column = lax.broadcasted_iota(jnp.int32, (TOKENS, TOKENS), 1)
    seen = key_row <= query_column

    def head(at, far_at):
        cols = lanes(at, HEAD)
        rows = pl.ds(pl.multiple_of(at, HEAD), HEAD)
        q_head = q[:, cols]
        d_head = d_attn[rows, :]
        keys = [k[:, cols]]
        values = [v[:, cols]]
        if far_at is not None:
            far_cols = lanes(far_at, HEAD)
            keys.append(far_k[:, far_cols])
            values.append(far_v[:, far_cols])
        scores = [nt(key, q_head) * EXP2_SCALE for key in keys]
        scores[0] = jnp.where(seen, scores[0], -jnp.inf)
        row_max = functools.reduce(
            jnp.maximum, [jnp.max(score, axis=0, keepdims=True) for score in scores]
        )
        raised = [jnp.exp2(score - row_max) for score in scores]
        total = sum(jnp.sum(r, axis=0, keepdims=True) for r in raised)
        inverse = 1.0 / total
        probs = [r * inverse for r in raised]
        probs_low = [p.astype(BF16) for p in probs]
        d_probs = [nn(value, d_head) for value in values]
        row_dot = sum(
            jnp.sum(p * d, axis=0, keepdims=True) for p, d in zip(probs, d_probs)
        )
        d_scores = [(p * (d - row_dot)).astype(BF16) for p, d in zip(probs, d_probs)]
        att[rows, :] = sum(tn(value, p) for value, p in zip(values, probs_low)).astype(BF16)
        dq[rows, :] = (sum(tn(key, s) for key, s in zip(keys, d_scores)) * SCALE).astype(BF16)
        dk[:, cols] = (nn(d_scores[0], q_head) * SCALE).astype(BF16)
        dv[:, cols] = nt(probs_low[0], d_head).astype(BF16)
        if far_at is not None:
            dk_far[:, far_cols] = (nn(d_scores[1], q_head) * SCALE).astype(BF16)
            dv_far[:, far_cols] = nt(probs_low[1], d_head).astype(BF16)

    for copy in qkv_copies[0]:
        copy.wait()

    def first_heads(j, carry):
        for i in range(2):
            head(j * 256 + i * HEAD, None)
        return carry

    lax.fori_loop(0, 4, first_heads, 0)
    for copy in qkv_copies[1]:
        copy.wait()

    def pair_heads(j, carry):
        for c, ref in ((0, far_k), (1, far_v)):
            part = ref.at[:, lanes(j * 256, 256)]
            pltpu.make_async_copy(part, part, kv_recv_sem.at[j, c]).wait()
        for i in range(2):
            head(HALF + j * 256 + i * HEAD, j * 256 + i * HEAD)
        return carry

    lax.fori_loop(0, 4, pair_heads, 0)

    halves = ((0, first_start), (HALF, pair_start))

    d_low_send[:RANK] = nt(up_ref[1, :, lanes(pair_start, HALF)], dk_far[...])
    d_low_send[RANK:] = nt(up_ref[2, :, lanes(pair_start, HALF)], dv_far[...])
    d_low_copy = pltpu.make_async_remote_copy(
        src_ref=d_low_send,
        dst_ref=d_low_recv,
        send_sem=small_send_sem.at[1],
        recv_sem=small_recv_sem.at[1],
        device_id=previous,
        device_id_type=MESH,
    )
    d_low_copy.start()

    def send_tiles(kind, base, count, late):
        def send(j, carry):
            to = away(ctx, j, count == 32) + (base % 32)
            to_y = lax.rem(to + kind + (0 if late else 1), 2)
            to_dp = to_y * 2 + kind
            slot = to + (0 if late else LATE_SLOTS)

            @pl.when(jnp.logical_or(to != ctx, to_dp != dp))
            def _():
                pltpu.make_async_remote_copy(
                    src_ref=low.at[kind * SLOTS + slot],
                    dst_ref=parts.at[me],
                    send_sem=part_send_sem,
                    recv_sem=part_recv_sem,
                    device_id=(to_dp, to),
                    device_id_type=MESH,
                ).start()

            return carry

        lax.fori_loop(0, count, send, 0)

    low_o = sum(
        nn(down_o_ref[:, lanes(start, HALF)], att[at : at + HALF, :]) for at, start in halves
    ).astype(BF16)
    up_o = nn(low_o, og[...])
    for n in range(16):
        low[SLOTS + 16 + n] = stacked(tile_of(up_o, n), tile_of(up_o, n + 16))
    send_tiles(1, 16, 16, True)

    low_copy.wait()
    for at, start in halves:
        up = [
            nt(low_in[:RANK], dq[at : at + HALF, :]),
            nn(low_in[RANK : 2 * RANK], dk[:, at : at + HALF]),
            nn(low_in[2 * RANK :], dv[:, at : at + HALF]),
        ]
        if at:
            up[1] += nn(low_far[:RANK], dk_far[...])
            up[2] += nn(low_far[RANK:], dv_far[...])
        down_o = nt(dy_low, att[at : at + HALF, :])
        slot = LATE_SLOTS + start // TILE
        for n in range(HALF // TILE):
            low[slot + n] = stacked(tile_of(up[0], n), tile_of(up[1], n))
            low[SLOTS + slot + n] = stacked(tile_of(up[2], n), tile_of(down_o, n))
    send_tiles(0, 0, 16, False)
    send_tiles(1, 0, 16, False)

    d_low = [
        sum(nn(up_ref[0, :, lanes(start, HALF)], dq[at : at + HALF, :]) for at, start in halves)
    ]
    for c, near in ((1, dk), (2, dv)):
        d_low.append(
            sum(
                nt(up_ref[c, :, lanes(start, HALF)], near[:, at : at + HALF])
                for at, start in halves
            )
        )
    d_low_copy.wait()
    d_low[1] += d_low_recv[:RANK]
    d_low[2] += d_low_recv[RANK:]
    d_low = jnp.concatenate(d_low, axis=0).astype(BF16)
    d_low_ref[...] = d_low
    down = nn(d_low, hid[...])
    third = down[2 * RANK :]
    for n in range(32):
        low[n] = tile_of(down[: 2 * RANK], n).astype(BF16)
    for n in range(16):
        low[SLOTS + n] = stacked(tile_of(third, n), tile_of(third, n + 16))
    send_tiles(0, 0, 32, True)
    send_tiles(1, 0, 16, True)

    is_late = lax.rem(ctx + core, 2) == y_lo
    is_owner = jnp.logical_or(is_late, ctx < 16)
    slot = jnp.where(is_late, ctx, LATE_SLOTS + ctx)

    @pl.when(is_owner)
    def _():
        parts[me] = low[core * SLOTS + slot]
        arriving = parts.at[0 : DEVICES - 1]
        pltpu.make_async_copy(arriving, arriving, part_recv_sem).wait()

        def add(n, total):
            return total + parts[n].astype(F32)

        total = lax.fori_loop(0, DEVICES, add, jnp.zeros((16, TILE), F32), unroll=8)
        summed_ref[core, slot] = (total * GRAD_SCALE).astype(BF16)

        def spread(j, carry):
            to = away(ctx, j, True)
            to_y = lax.rem(y_lo + 1 + j // 32, 2)

            @pl.when(jnp.logical_or(to != ctx, to_y != y_lo))
            def _():
                pltpu.make_async_remote_copy(
                    src_ref=summed_ref.at[core, slot],
                    dst_ref=summed_ref.at[core, slot],
                    send_sem=sum_send_sem,
                    recv_sem=sum_recv_sem,
                    device_id=(to_y * 2 + core, to),
                    device_id_type=MESH,
                ).start()

            return carry

        lax.fori_loop(0, 64, spread, 0)
        arriving = parts.at[0 : SLOTS - 1]
        pltpu.make_async_copy(arriving, arriving, sum_recv_sem).wait()

    @pl.when(jnp.logical_not(is_owner))
    def _():
        arriving = parts.at[0:SLOTS]
        pltpu.make_async_copy(arriving, arriving, sum_recv_sem).wait()

    last = pltpu.make_async_remote_copy(
        src_ref=summed_ref.at[core],
        dst_ref=summed_ref.at[core],
        send_sem=last_sems.at[0],
        recv_sem=last_sems.at[1],
        device_id=(y_lo * 2 + 1 - core, ctx),
        device_id_type=MESH,
    )
    last.start()

    @pl.when(is_owner)
    def _():
        sent = low.at[0 : 2 * SLOTS - 1]
        pltpu.make_async_copy(sent, sent, part_send_sem).wait()
        sent = low.at[0:63]
        pltpu.make_async_copy(sent, sent, sum_send_sem).wait()

    @pl.when(jnp.logical_not(is_owner))
    def _():
        pltpu.make_async_copy(low, low, part_send_sem).wait()

    for copy in kv_copies:
        copy.wait_send()
    last.wait()


def attention_part(hidden, projected, gradient, weight, down, up, down_o, up_o):
    half = VMEM((TOKENS, HALF), BF16)
    whole = VMEM((TOKENS, HEADS_WIDTH), BF16)
    flipped = VMEM((HEADS_WIDTH, TOKENS), BF16)
    wide = VMEM((TOKENS, MODEL), BF16)
    anywhere = pl.BlockSpec(memory_space=pl.ANY)
    resident = pl.BlockSpec(memory_space=VMEM)
    return pl.pallas_call(
        attention_kernel,
        out_shape=(
            jax.ShapeDtypeStruct((3 * RANK, TOKENS), BF16),
            jax.ShapeDtypeStruct((2, SLOTS, 16, TILE), BF16),
        ),
        in_specs=[anywhere] * 4 + [resident] * 4,
        out_specs=(resident, resident),
        scratch_shapes=[
            wide,
            whole,
            whole,
            whole,
            wide,
            VMEM((HEADS_WIDTH, MODEL), BF16),
            half,
            half,
            flipped,
            flipped,
            flipped,
            whole,
            whole,
            half,
            half,
            VMEM((2 * RANK, TOKENS), BF16),
            VMEM((2 * RANK, TOKENS), BF16),
            VMEM((2 * RANK, TOKENS), F32),
            VMEM((2 * RANK, TOKENS), F32),
            VMEM((2 * SLOTS, 16, TILE), BF16),
            VMEM((DEVICES, 16, TILE), BF16),
            DMA((2,)),
            DMA((4,)),
            DMA((2, 3)),
            DMA((4, 2)),
            DMA((4, 2)),
            DMA((2,)),
            DMA((2,)),
            DMA,
            DMA,
            DMA,
            DMA,
            DMA((2,)),
        ],
        compiler_params=pltpu.CompilerParams(
            collective_id=0, has_side_effects=True, vmem_limit_bytes=56 << 20
        ),
    )(hidden, projected, gradient, weight, down, up, down_o, up_o)


def finish_kernel(
    summed_ref,
    d_low_ref,
    down_ref,
    input_hbm,
    grad_down_ref,
    grad_up_ref,
    down_o_ref,
    up_o_ref,
    result,
    sems,
):
    copies = []
    for n in range(4):
        cols = slice(n * HALF, (n + 1) * HALF)
        result[:, cols] = (2.0 * tn(d_low_ref[...], down_ref[:, cols])).astype(BF16)
        copy = pltpu.make_async_copy(result.at[:, cols], input_hbm.at[0, :, cols], sems.at[n])
        copy.start()
        copies.append(copy)

    def halves_of(kind, slot):
        tile = summed_ref[kind, slot].astype(F32)
        return tile[:RANK].astype(BF16), tile[RANK:].astype(BF16)

    for n in range(32):
        cols = slice(n * TILE, (n + 1) * TILE)
        grad_down_ref[0, :, cols], grad_down_ref[1, :, cols] = halves_of(0, n)
    for n in range(16):
        cols = slice(n * TILE, (n + 1) * TILE)
        later = slice(HEADS_WIDTH + n * TILE, HEADS_WIDTH + (n + 1) * TILE)
        grad_down_ref[2, :, cols], grad_down_ref[2, :, later] = halves_of(1, n)
        up_o_ref[:, cols], up_o_ref[:, later] = halves_of(1, 16 + n)
        grad_up_ref[0, :, cols], grad_up_ref[1, :, cols] = halves_of(0, LATE_SLOTS + n)
        grad_up_ref[2, :, cols], down_o_ref[:, cols] = halves_of(1, LATE_SLOTS + n)
    for copy in copies:
        copy.wait()


def finish_part(summed, d_low, down):
    resident = pl.BlockSpec(memory_space=VMEM)
    return pl.pallas_call(
        finish_kernel,
        out_shape=(
            jax.ShapeDtypeStruct((1, TOKENS, MODEL), BF16),
            jax.ShapeDtypeStruct((3, RANK, MODEL), BF16),
            jax.ShapeDtypeStruct((3, RANK, HEADS_WIDTH), BF16),
            jax.ShapeDtypeStruct((RANK, HEADS_WIDTH), BF16),
            jax.ShapeDtypeStruct((RANK, MODEL), BF16),
        ),
        in_specs=[resident] * 3,
        out_specs=(pl.BlockSpec(memory_space=pl.ANY),) + (resident,) * 4,
        scratch_shapes=[VMEM((TOKENS, MODEL), BF16), DMA((4,))],
        compiler_params=pltpu.CompilerParams(vmem_limit_bytes=32 << 20),
    )(summed, d_low, down)


def per_device(hidden, projected, gradient, weight, down, up, down_o, up_o):
    down = down.reshape(3 * RANK, MODEL)
    d_low, summed = attention_part(hidden, projected, gradient, weight, down, up, down_o, up_o)
    return finish_part(summed, d_low, down)


def solution(mesh):
    in_specs = (
        P("dp", "ctx", None),
        P(None, "dp", "ctx", None),
        P("dp", "ctx", None),
        P(),
        P(),
        P(),
        P(),
        P(),
    )
    out_specs = (P("dp", "ctx", None), P(), P(), P(), P())
    return jax.shard_map(
        per_device, mesh=mesh, in_specs=in_specs, out_specs=out_specs, check_vma=False
    )
```

```python
import functools
import math

import jax
import jax.numpy as jnp
from jax import lax
from jax.experimental import pallas as pl
from jax.experimental.pallas import tpu as pltpu
from jax.sharding import PartitionSpec as P

MESH = pl.DeviceIdType.MESH
DMA = pltpu.SemaphoreType.DMA
VMEM = pltpu.VMEM
F32 = jnp.float32
BF16 = jnp.bfloat16

TOKENS = 256
MODEL = 4096
HEADS_WIDTH = 2048
HALF = 1024
HEAD = 128
RANK = 8
CTX = 32
SCALE = 1.0 / math.sqrt(HEAD)
EXP2_SCALE = SCALE * math.log2(math.e)
GRAD_SCALE = 2.0 / 32768
OW_BLOCK = 512

TILE = 128
LATE_SLOTS = 32
SLOTS = 48
AHEAD = 768
BACK = 256
FIRST_STEP = 2
DEVICES = 128


def nn(a, b):
    return lax.dot_general(a, b, (((1,), (0,)), ((), ())), preferred_element_type=F32)


def nt(a, b):
    return lax.dot_general(a, b, (((1,), (1,)), ((), ())), preferred_element_type=F32)


def tn(a, b):
    return lax.dot_general(a, b, (((0,), (0,)), ((), ())), preferred_element_type=F32)


def lanes(start, size):
    return pl.ds(pl.multiple_of(start, 128), size)


def stacked(top, bottom):
    return jnp.concatenate([top, bottom], axis=0).astype(BF16)


def tile_of(value, n):
    return value[:, n * TILE : (n + 1) * TILE]


def attention_kernel(
    hidden_hbm,
    projected_hbm,
    gradient_hbm,
    weight_hbm,
    down_ref,
    up_ref,
    down_o_ref,
    up_o_ref,
    d_low_ref,
    summed_ref,
    hid,
    q,
    k,
    v,
    og,
    ow,
    far_k,
    far_v,
    next_qkv,
    next_d,
    d_attn,
    att,
    dq,
    dk,
    dv,
    dk_far,
    dv_far,
    next_att,
    next_dq,
    next_dk,
    next_dv,
    dk_cross,
    dv_cross,
    thin,
    far_low,
    next_thin,
    totals,
    far_send,
    far_recv,
    next_send,
    next_recv,
    low,
    parts,
    in_sem,
    ow_sem,
    qkv_sem,
    kv_send_sem,
    kv_recv_sem,
    back_send_sem,
    back_recv_sem,
    small_send_sem,
    small_recv_sem,
    part_send_sem,
    part_recv_sem,
    sum_send_sem,
    sum_recv_sem,
    last_sems,
):
    dp = lax.axis_index("dp")
    ctx = lax.axis_index("ctx")
    following = (dp, lax.rem(ctx + 1, CTX))
    previous = (dp, lax.rem(ctx + CTX - 1, CTX))
    parity = lax.rem(ctx, 2)
    first_start = parity * HALF
    pair_start = (1 - parity) * HALF
    core = lax.rem(dp, 2)
    y_lo = dp // 2
    me = dp * CTX + ctx

    def remote(source, target, send_sem, recv_sem, device):
        return pltpu.make_async_remote_copy(
            src_ref=source,
            dst_ref=target,
            send_sem=send_sem,
            recv_sem=recv_sem,
            device_id=device,
            device_id_type=MESH,
        )

    def ow_copy(block):
        start = first_start if block < 2 else pair_start
        row = start + block % 2 * OW_BLOCK
        return pltpu.make_async_copy(
            weight_hbm.at[pl.ds(pl.multiple_of(row, OW_BLOCK), OW_BLOCK), :],
            ow.at[block * OW_BLOCK : (block + 1) * OW_BLOCK, :],
            ow_sem.at[block],
        )

    og_copy = pltpu.make_async_copy(gradient_hbm.at[0], og, in_sem.at[0])
    hid_copy = pltpu.make_async_copy(hidden_hbm.at[0], hid, in_sem.at[1])
    qkv_copies = [
        [
            pltpu.make_async_copy(
                projected_hbm.at[c, 0, :, lanes(start, HALF)],
                ref.at[:, at * HALF : (at + 1) * HALF],
                qkv_sem.at[at, c],
            )
            for c, ref in enumerate((q, k, v))
        ]
        for at, start in enumerate((first_start, pair_start))
    ]
    og_copy.start()
    ow_copy(3).start()

    barrier = pltpu.get_barrier_semaphore()

    def greet(n, carry):
        other = lax.rem(ctx + n, CTX)
        for other_dp in range(4):

            @pl.when(jnp.logical_or(n != 0, other_dp != dp))
            def _():
                pl.semaphore_signal(
                    barrier, inc=1, device_id=(other_dp, other), device_id_type=MESH
                )

        return carry

    lax.fori_loop(0, CTX, greet, 0)
    pl.semaphore_wait(barrier, DEVICES - 1)
    sent = []
    for j in range(3):
        for c, ref in ((0, far_k), (1, far_v)):
            copy = remote(
                projected_hbm.at[c + 1, 0, :, lanes(first_start + j * 256, 256)],
                ref.at[:, j * 256 : (j + 1) * 256],
                kv_send_sem.at[j, c],
                kv_recv_sem.at[j, c],
                following,
            )
            copy.start()
            sent.append(copy)
    back = [
        remote(
            projected_hbm.at[c, 0, :, lanes(pair_start + AHEAD, BACK)],
            next_qkv.at[c],
            back_send_sem.at[c],
            back_recv_sem.at[c],
            previous,
        )
        for c in range(3)
    ]
    for copy in back:
        copy.start()

    ow_copy(0).start()
    hid_copy.start()
    og_copy.wait()
    dy_low = nt(up_o_ref[...], og[...]).astype(BF16)

    def project(block):
        ow_copy(block).wait()
        start = first_start if block < 2 else pair_start
        column = start + block % 2 * OW_BLOCK
        rows = slice(block * OW_BLOCK, (block + 1) * OW_BLOCK)
        through_adapter = tn(down_o_ref[:, lanes(column, OW_BLOCK)], dy_low)
        d_attn[rows, :] = (nt(ow[rows, :], og[...]) + 2.0 * through_adapter).astype(BF16)

    ow_copy(1).start()
    project(3)
    d_copy = remote(
        d_attn.at[HALF + AHEAD : HEADS_WIDTH, :],
        next_d,
        back_send_sem.at[3],
        back_recv_sem.at[3],
        previous,
    )
    d_copy.start()
    back.append(d_copy)
    for copy in qkv_copies[0]:
        copy.start()
    ow_copy(2).start()
    for copy in qkv_copies[1]:
        copy.start()

    hid_copy.wait()
    low_in = nt(down_ref[...], hid[...]).astype(BF16)
    thin[...] = jnp.concatenate([dy_low, low_in], axis=0)
    thin_copies = [
        remote(thin, next_thin, small_send_sem.at[0], small_recv_sem.at[0], previous),
        remote(
            thin.at[2 * RANK :], far_low, small_send_sem.at[1], small_recv_sem.at[1], following
        ),
    ]
    for copy in thin_copies:
        copy.start()
    project(0)
    project(1)
    project(2)

    key_row = lax.broadcasted_iota(jnp.int32, (TOKENS, TOKENS), 0)
    query_column = lax.broadcasted_iota(jnp.int32, (TOKENS, TOKENS), 1)
    seen = key_row <= query_column

    def head(q_head, d_head, keys, values):
        scores = [nt(key, q_head) * EXP2_SCALE for key in keys]
        scores[0] = jnp.where(seen, scores[0], -jnp.inf)
        row_max = functools.reduce(
            jnp.maximum, [jnp.max(score, axis=0, keepdims=True) for score in scores]
        )
        raised = [jnp.exp2(score - row_max) for score in scores]
        total = sum(jnp.sum(r, axis=0, keepdims=True) for r in raised)
        inverse = 1.0 / total
        probs = [r * inverse for r in raised]
        probs_low = [p.astype(BF16) for p in probs]
        d_probs = [nn(value, d_head) for value in values]
        row_dot = sum(
            jnp.sum(p * d, axis=0, keepdims=True) for p, d in zip(probs, d_probs)
        )
        d_scores = [(p * (d - row_dot)).astype(BF16) for p, d in zip(probs, d_probs)]
        attended = sum(tn(value, p) for value, p in zip(values, probs_low)).astype(BF16)
        d_query = (sum(tn(key, s) for key, s in zip(keys, d_scores)) * SCALE).astype(BF16)
        d_keys = [(nn(s, q_head) * SCALE).astype(BF16) for s in d_scores]
        d_values = [nt(p, d_head).astype(BF16) for p in probs_low]
        return attended, d_query, d_keys, d_values

    for copy in qkv_copies[0]:
        copy.wait()

    def first_heads(j, carry):
        for i in range(FIRST_STEP):
            at = (j * FIRST_STEP + i) * HEAD
            cols, rows = lanes(at, HEAD), pl.ds(pl.multiple_of(at, HEAD), HEAD)
            att[rows, :], dq[rows, :], d_keys, d_values = head(
                q[:, cols], d_attn[rows, :], [k[:, cols]], [v[:, cols]]
            )
            dk[:, cols], dv[:, cols] = d_keys[0], d_values[0]
        return carry

    lax.fori_loop(0, 8 // FIRST_STEP, first_heads, 0)

    first = lanes(first_start, HALF)
    totals[:RANK] = nn(up_ref[0, :, first], dq[:HALF, :])
    totals[RANK : 2 * RANK] = nt(up_ref[1, :, first], dk[:, :HALF])
    totals[2 * RANK : 3 * RANK] = nt(up_ref[2, :, first], dv[:, :HALF])
    totals[3 * RANK :] = nn(down_o_ref[:, first], att[:HALF, :])
    first_slot = LATE_SLOTS + first_start // TILE
    pair_slot = LATE_SLOTS + pair_start // TILE

    def pack(slot, ups, down_o):
        for n in range(down_o.shape[1] // TILE):
            low[slot + n] = stacked(tile_of(ups[0], n), tile_of(ups[1], n))
            low[SLOTS + slot + n] = stacked(tile_of(ups[2], n), tile_of(down_o, n))

    def ups_of(low_in_all, rows, cols, d_query, d_key, d_value):
        return [
            nt(low_in_all[:RANK], d_query[rows, :]),
            nn(low_in_all[RANK : 2 * RANK], d_key[:, cols]),
            nn(low_in_all[2 * RANK :], d_value[:, cols]),
        ]

    ahead = slice(0, AHEAD)
    pack(first_slot, ups_of(low_in, ahead, ahead, dq, dk, dv), nt(dy_low, att[:AHEAD, :]))
    for n in (6, 7):
        low[pair_slot + n] = jnp.zeros((16, TILE), BF16)
        low[SLOTS + pair_slot + n] = jnp.zeros((16, TILE), BF16)

    for copy in qkv_copies[1]:
        copy.wait()

    def arrived(ref, sem):
        pltpu.make_async_copy(ref, ref, sem).wait()

    whole = slice(0, BACK)
    turned = lanes(first_start + AHEAD, BACK)

    def next_device_heads():
        for c in range(3):
            arrived(next_qkv.at[c], back_recv_sem.at[c])
        arrived(next_d, back_recv_sem.at[3])
        arrived(next_thin, small_recv_sem.at[0])
        for i in range(2):
            part = slice(i * HEAD, (i + 1) * HEAD)
            cols = slice(AHEAD + i * HEAD, AHEAD + (i + 1) * HEAD)
            next_att[part, :], next_dq[part, :], d_keys, d_values = head(
                next_qkv[0, :, part],
                next_d[part, :],
                [next_qkv[1, :, part], k[:, cols]],
                [next_qkv[2, :, part], v[:, cols]],
            )
            next_dk[:, part], dk_cross[:, part] = d_keys
            next_dv[:, part], dv_cross[:, part] = d_values
        next_send[:RANK] = nn(up_ref[0, :, turned], next_dq[...])
        next_send[RANK : 2 * RANK] = nt(up_ref[1, :, turned], next_dk[...])
        next_send[2 * RANK : 3 * RANK] = nt(up_ref[2, :, turned], next_dv[...])
        next_send[3 * RANK :] = nn(down_o_ref[:, turned], next_att[...])
        next_copy.start()
        totals[RANK : 2 * RANK] += nt(up_ref[1, :, turned], dk_cross[...])
        totals[2 * RANK : 3 * RANK] += nt(up_ref[2, :, turned], dv_cross[...])
        own = ups_of(
            low_in, slice(AHEAD, HALF), slice(AHEAD, HALF), dq, dk, dv
        )
        other = ups_of(next_thin[RANK:], whole, whole, next_dq, next_dk, next_dv)
        ups = [a + b for a, b in zip(own, other)]
        ups[1] += nn(low_in[RANK : 2 * RANK], dk_cross[...])
        ups[2] += nn(low_in[2 * RANK :], dv_cross[...])
        down_o = nt(dy_low, att[AHEAD:HALF, :]) + nt(next_thin[:RANK], next_att[...])
        pack(first_slot + 6, ups, down_o)

    next_copy = remote(
        next_send, next_recv, small_send_sem.at[3], small_recv_sem.at[3], following
    )

    def pair_heads(j, carry):
        @pl.when(j == 2)
        def _():
            next_device_heads()

        for c, ref in ((0, far_k), (1, far_v)):
            arrived(ref.at[:, lanes(j * 256, 256)], kv_recv_sem.at[j, c])
        for i in range(2):
            far_cols = lanes(j * 256 + i * HEAD, HEAD)
            at = HALF + j * 256 + i * HEAD
            cols, rows = lanes(at, HEAD), pl.ds(pl.multiple_of(at, HEAD), HEAD)
            att[rows, :], dq[rows, :], d_keys, d_values = head(
                q[:, cols],
                d_attn[rows, :],
                [k[:, cols], far_k[:, far_cols]],
                [v[:, cols], far_v[:, far_cols]],
            )
            dk[:, cols], dk_far[:, far_cols] = d_keys
            dv[:, cols], dv_far[:, far_cols] = d_values
        return carry

    lax.fori_loop(0, 3, pair_heads, 0)

    pair = lanes(pair_start, AHEAD)
    far_send[:RANK] = nt(up_ref[1, :, pair], dk_far[...])
    far_send[RANK:] = nt(up_ref[2, :, pair], dv_far[...])
    far_copy = remote(far_send, far_recv, small_send_sem.at[2], small_recv_sem.at[2], previous)
    far_copy.start()

    z_place = [lax.rem(ctx + 2 + n, 4) for n in range(4)]
    x_place = lax.rem(ctx // 4, 4)
    y_place = ctx // 16

    def send_tiles(kind, base, count, late):
        y_of = [lax.rem(z + kind + (0 if late else 1), 2) for z in z_place]

        def send(j, carry):
            line = lax.rem(x_place + 2 + j, 4) * 4
            if count == 32:
                line += lax.rem(y_place + 1 + j // 4, 2) * 16
            else:
                line += base % 32
            for z, to_y in zip(z_place, y_of):
                to = line + z
                to_dp = to_y * 2 + kind

                @pl.when(jnp.logical_or(to != ctx, to_dp != dp))
                def _():
                    remote(
                        low.at[kind * SLOTS + to + (0 if late else LATE_SLOTS)],
                        parts.at[me],
                        part_send_sem,
                        part_recv_sem,
                        (to_dp, to),
                    ).start()

            return carry

        lax.fori_loop(0, count // 4, send, 0)

    pair_rows = slice(HALF, HALF + AHEAD)
    arrived(next_recv, small_recv_sem.at[3])
    low_o = (
        totals[3 * RANK :]
        + next_recv[3 * RANK :]
        + nn(down_o_ref[:, pair], att[pair_rows, :])
    ).astype(BF16)
    up_o = nn(low_o, og[...])
    for n in range(16):
        low[SLOTS + 16 + n] = stacked(tile_of(up_o, n), tile_of(up_o, n + 16))
    send_tiles(1, 16, 16, True)

    arrived(far_low, small_recv_sem.at[1])
    ups = ups_of(low_in, pair_rows, pair_rows, dq, dk, dv)
    ups[1] += nn(far_low[:RANK], dk_far[...])
    ups[2] += nn(far_low[RANK:], dv_far[...])
    pack(pair_slot, ups, nt(dy_low, att[pair_rows, :]))
    send_tiles(0, 0, 16, False)
    send_tiles(1, 0, 16, False)

    d_low = totals[: 3 * RANK] + next_recv[: 3 * RANK]
    d_low += jnp.concatenate(
        [
            nn(up_ref[0, :, pair], dq[pair_rows, :]),
            nt(up_ref[1, :, pair], dk[:, pair_rows]),
            nt(up_ref[2, :, pair], dv[:, pair_rows]),
        ],
        axis=0,
    )
    arrived(far_recv, small_recv_sem.at[2])
    d_low += jnp.concatenate([jnp.zeros((RANK, TOKENS), F32), far_recv[...]], axis=0)
    d_low = d_low.astype(BF16)
    d_low_ref[...] = d_low
    down = nn(d_low, hid[...])
    third = down[2 * RANK :]
    for n in range(32):
        low[n] = tile_of(down[: 2 * RANK], n).astype(BF16)
    for n in range(16):
        low[SLOTS + n] = stacked(tile_of(third, n), tile_of(third, n + 16))
    send_tiles(0, 0, 32, True)
    send_tiles(1, 0, 16, True)

    is_late = lax.rem(ctx + core, 2) == y_lo
    is_owner = jnp.logical_or(is_late, ctx < 16)
    slot = jnp.where(is_late, ctx, LATE_SLOTS + ctx)

    @pl.when(is_owner)
    def _():
        parts[me] = low[core * SLOTS + slot]
        arrived(parts.at[0 : DEVICES - 1], part_recv_sem)

        def add(n, total):
            return total + parts[n].astype(F32)

        total = lax.fori_loop(0, DEVICES, add, jnp.zeros((16, TILE), F32), unroll=8)
        summed_ref[core, slot] = (total * GRAD_SCALE).astype(BF16)

        def spread(j, carry):
            line = lax.rem(x_place + 2 + j, 4) * 4 + lax.rem(y_place + 1 + j // 4 % 2, 2) * 16
            to_y = lax.rem(y_lo + 1 + j // 8, 2)
            for z in z_place:
                to = line + z

                @pl.when(jnp.logical_or(to != ctx, to_y != y_lo))
                def _():
                    remote(
                        summed_ref.at[core, slot],
                        summed_ref.at[core, slot],
                        sum_send_sem,
                        sum_recv_sem,
                        (to_y * 2 + core, to),
                    ).start()

            return carry

        lax.fori_loop(0, 16, spread, 0)
        arrived(parts.at[0 : SLOTS - 1], sum_recv_sem)

    @pl.when(jnp.logical_not(is_owner))
    def _():
        arrived(parts.at[0:SLOTS], sum_recv_sem)

    last = remote(
        summed_ref.at[core],
        summed_ref.at[core],
        last_sems.at[0],
        last_sems.at[1],
        (y_lo * 2 + 1 - core, ctx),
    )
    last.start()

    @pl.when(is_owner)
    def _():
        arrived(low.at[0 : 2 * SLOTS - 1], part_send_sem)
        arrived(low.at[0:63], sum_send_sem)

    @pl.when(jnp.logical_not(is_owner))
    def _():
        arrived(low, part_send_sem)

    for copy in sent + back + thin_copies + [far_copy, next_copy]:
        copy.wait_send()
    last.wait()


def attention_part(hidden, projected, gradient, weight, down, up, down_o, up_o):
    ahead = VMEM((TOKENS, AHEAD), BF16)
    square = VMEM((TOKENS, BACK), BF16)
    whole = VMEM((TOKENS, HEADS_WIDTH), BF16)
    flipped = VMEM((HEADS_WIDTH, TOKENS), BF16)
    wide = VMEM((TOKENS, MODEL), BF16)
    anywhere = pl.BlockSpec(memory_space=pl.ANY)
    resident = pl.BlockSpec(memory_space=VMEM)
    return pl.pallas_call(
        attention_kernel,
        out_shape=(
            jax.ShapeDtypeStruct((3 * RANK, TOKENS), BF16),
            jax.ShapeDtypeStruct((2, SLOTS, 16, TILE), BF16),
        ),
        in_specs=[anywhere] * 4 + [resident] * 4,
        out_specs=(resident, resident),
        scratch_shapes=[
            wide,
            whole,
            whole,
            whole,
            wide,
            VMEM((HEADS_WIDTH, MODEL), BF16),
            ahead,
            ahead,
            VMEM((3, TOKENS, BACK), BF16),
            square,
            flipped,
            flipped,
            flipped,
            whole,
            whole,
            ahead,
            ahead,
            square,
            square,
            square,
            square,
            square,
            square,
            VMEM((4 * RANK, TOKENS), BF16),
            VMEM((2 * RANK, TOKENS), BF16),
            VMEM((4 * RANK, TOKENS), BF16),
            VMEM((4 * RANK, TOKENS), F32),
            VMEM((2 * RANK, TOKENS), F32),
            VMEM((2 * RANK, TOKENS), F32),
            VMEM((4 * RANK, TOKENS), F32),
            VMEM((4 * RANK, TOKENS), F32),
            VMEM((2 * SLOTS, 16, TILE), BF16),
            VMEM((DEVICES, 16, TILE), BF16),
            DMA((2,)),
            DMA((4,)),
            DMA((2, 3)),
            DMA((3, 2)),
            DMA((3, 2)),
            DMA((4,)),
            DMA((4,)),
            DMA((4,)),
            DMA((4,)),
            DMA,
            DMA,
            DMA,
            DMA,
            DMA((2,)),
        ],
        compiler_params=pltpu.CompilerParams(
            collective_id=0, has_side_effects=True, vmem_limit_bytes=56 << 20
        ),
    )(hidden, projected, gradient, weight, down, up, down_o, up_o)


def finish_kernel(
    summed_hbm,
    d_low_hbm,
    down_hbm,
    input_hbm,
    grad_down_ref,
    grad_up_ref,
    down_o_ref,
    up_o_ref,
    summed,
    d_low,
    down,
    result,
    in_sems,
    sems,
):
    fetches = [
        pltpu.make_async_copy(source, target, in_sems.at[n])
        for n, (source, target) in enumerate(
            ((d_low_hbm, d_low), (down_hbm, down), (summed_hbm, summed))
        )
    ]
    for fetch in fetches:
        fetch.start()
    fetches[0].wait()
    fetches[1].wait()
    copies = []
    for n in range(4):
        rows = slice(n * 64, (n + 1) * 64)
        result[rows, :] = (2.0 * tn(d_low[:, rows], down[...])).astype(BF16)
        copy = pltpu.make_async_copy(result.at[rows, :], input_hbm.at[0, rows, :], sems.at[n])
        copy.start()
        copies.append(copy)
    fetches[2].wait()

    def halves_of(kind, slot):
        tile = summed[kind, slot].astype(F32)
        return tile[:RANK].astype(BF16), tile[RANK:].astype(BF16)

    for n in range(32):
        cols = slice(n * TILE, (n + 1) * TILE)
        grad_down_ref[0, :, cols], grad_down_ref[1, :, cols] = halves_of(0, n)
    for n in range(16):
        cols = slice(n * TILE, (n + 1) * TILE)
        later = slice(HEADS_WIDTH + n * TILE, HEADS_WIDTH + (n + 1) * TILE)
        grad_down_ref[2, :, cols], grad_down_ref[2, :, later] = halves_of(1, n)
        up_o_ref[:, cols], up_o_ref[:, later] = halves_of(1, 16 + n)
        grad_up_ref[0, :, cols], grad_up_ref[1, :, cols] = halves_of(0, LATE_SLOTS + n)
        grad_up_ref[2, :, cols], down_o_ref[:, cols] = halves_of(1, LATE_SLOTS + n)
    for copy in copies:
        copy.wait()


def finish_part(summed, d_low, down):
    resident = pl.BlockSpec(memory_space=VMEM)
    anywhere = pl.BlockSpec(memory_space=pl.ANY)
    return pl.pallas_call(
        finish_kernel,
        out_shape=(
            jax.ShapeDtypeStruct((1, TOKENS, MODEL), BF16),
            jax.ShapeDtypeStruct((3, RANK, MODEL), BF16),
            jax.ShapeDtypeStruct((3, RANK, HEADS_WIDTH), BF16),
            jax.ShapeDtypeStruct((RANK, HEADS_WIDTH), BF16),
            jax.ShapeDtypeStruct((RANK, MODEL), BF16),
        ),
        in_specs=[anywhere] * 3,
        out_specs=(anywhere,) + (resident,) * 4,
        scratch_shapes=[
            VMEM((2, SLOTS, 16, TILE), BF16),
            VMEM((3 * RANK, TOKENS), BF16),
            VMEM((3 * RANK, MODEL), BF16),
            VMEM((TOKENS, MODEL), BF16),
            DMA((3,)),
            DMA((4,)),
        ],
        compiler_params=pltpu.CompilerParams(vmem_limit_bytes=60 << 20),
    )(summed, d_low, down)


def per_device(hidden, projected, gradient, weight, down, up, down_o, up_o):
    down = down.reshape(3 * RANK, MODEL)
    d_low, summed = attention_part(hidden, projected, gradient, weight, down, up, down_o, up_o)
    return finish_part(summed, d_low, down)


def solution(mesh):
    in_specs = (
        P("dp", "ctx", None),
        P(None, "dp", "ctx", None),
        P("dp", "ctx", None),
        P(),
        P(),
        P(),
        P(),
        P(),
    )
    out_specs = (P("dp", "ctx", None), P(), P(), P(), P())
    return jax.shard_map(
        per_device, mesh=mesh, in_specs=in_specs, out_specs=out_specs, check_vma=False
    )
```

```python
import functools
import math

import jax
import jax.numpy as jnp
from jax import lax
from jax.experimental import pallas as pl
from jax.experimental.pallas import tpu as pltpu
from jax.sharding import PartitionSpec as P

MESH = pl.DeviceIdType.MESH
DMA = pltpu.SemaphoreType.DMA
VMEM = pltpu.VMEM
F32 = jnp.float32
BF16 = jnp.bfloat16

TOKENS = 256
MODEL = 4096
HEADS_WIDTH = 2048
HALF = 1024
HEAD = 128
RANK = 8
CTX = 32
SCALE = 1.0 / math.sqrt(HEAD)
EXP2_SCALE = SCALE * math.log2(math.e)
GRAD_SCALE = 2.0 / 32768
OW_BLOCK = 512

TILE = 128
LATE_SLOTS = 32
SLOTS = 48
AHEAD = 768
BACK = 256
FIRST_STEP = 2
DEVICES = 128
CHIPS = 64


def nn(a, b):
    return lax.dot_general(a, b, (((1,), (0,)), ((), ())), preferred_element_type=F32)


def nt(a, b):
    return lax.dot_general(a, b, (((1,), (1,)), ((), ())), preferred_element_type=F32)


def tn(a, b):
    return lax.dot_general(a, b, (((0,), (0,)), ((), ())), preferred_element_type=F32)


def lanes(start, size):
    return pl.ds(pl.multiple_of(start, 128), size)


def stacked(top, bottom):
    return jnp.concatenate([top, bottom], axis=0).astype(BF16)


def tile_of(value, n):
    return value[:, n * TILE : (n + 1) * TILE]


def attention_kernel(
    hidden_hbm,
    projected_hbm,
    gradient_hbm,
    weight_hbm,
    down_ref,
    up_ref,
    down_o_ref,
    up_o_ref,
    d_low_ref,
    summed_ref,
    hid,
    q,
    k,
    v,
    og,
    ow,
    far_k,
    far_v,
    next_qkv,
    next_d,
    d_attn,
    att,
    dq,
    dk,
    dv,
    dk_far,
    dv_far,
    next_att,
    next_dq,
    next_dk,
    next_dv,
    dk_cross,
    dv_cross,
    thin,
    far_low,
    next_thin,
    totals,
    far_send,
    far_recv,
    next_send,
    next_recv,
    low,
    parts,
    in_sem,
    ow_sem,
    qkv_sem,
    kv_send_sem,
    kv_recv_sem,
    back_send_sem,
    back_recv_sem,
    small_send_sem,
    small_recv_sem,
    part_send_sem,
    part_recv_sem,
    sum_send_sem,
    sum_recv_sem,
    last_sems,
    sibling,
    sibling_sems,
):
    dp = lax.axis_index("dp")
    ctx = lax.axis_index("ctx")
    following = (dp, lax.rem(ctx + 1, CTX))
    previous = (dp, lax.rem(ctx + CTX - 1, CTX))
    parity = lax.rem(ctx, 2)
    first_start = parity * HALF
    pair_start = (1 - parity) * HALF
    core = lax.rem(dp, 2)
    y_lo = dp // 2
    me = dp * CTX + ctx

    def remote(source, target, send_sem, recv_sem, device):
        return pltpu.make_async_remote_copy(
            src_ref=source,
            dst_ref=target,
            send_sem=send_sem,
            recv_sem=recv_sem,
            device_id=device,
            device_id_type=MESH,
        )

    def ow_copy(block):
        start = first_start if block < 2 else pair_start
        row = start + block % 2 * OW_BLOCK
        return pltpu.make_async_copy(
            weight_hbm.at[pl.ds(pl.multiple_of(row, OW_BLOCK), OW_BLOCK), :],
            ow.at[block * OW_BLOCK : (block + 1) * OW_BLOCK, :],
            ow_sem.at[block],
        )

    og_copy = pltpu.make_async_copy(gradient_hbm.at[0], og, in_sem.at[0])
    hid_copy = pltpu.make_async_copy(hidden_hbm.at[0], hid, in_sem.at[1])
    qkv_copies = [
        [
            pltpu.make_async_copy(
                projected_hbm.at[c, 0, :, lanes(start, HALF)],
                ref.at[:, at * HALF : (at + 1) * HALF],
                qkv_sem.at[at, c],
            )
            for c, ref in enumerate((q, k, v))
        ]
        for at, start in enumerate((first_start, pair_start))
    ]
    og_copy.start()
    ow_copy(3).start()

    barrier = pltpu.get_barrier_semaphore()

    def greet(n, carry):
        other = lax.rem(ctx + n, CTX)
        for other_dp in range(4):

            @pl.when(jnp.logical_or(n != 0, other_dp != dp))
            def _():
                pl.semaphore_signal(
                    barrier, inc=1, device_id=(other_dp, other), device_id_type=MESH
                )

        return carry

    lax.fori_loop(0, CTX, greet, 0)
    pl.semaphore_wait(barrier, DEVICES - 1)
    sent = []
    for j in range(3):
        for c, ref in ((0, far_k), (1, far_v)):
            copy = remote(
                projected_hbm.at[c + 1, 0, :, lanes(first_start + j * 256, 256)],
                ref.at[:, j * 256 : (j + 1) * 256],
                kv_send_sem.at[j, c],
                kv_recv_sem.at[j, c],
                following,
            )
            copy.start()
            sent.append(copy)
    back = [
        remote(
            projected_hbm.at[c, 0, :, lanes(pair_start + AHEAD, BACK)],
            next_qkv.at[c],
            back_send_sem.at[c],
            back_recv_sem.at[c],
            previous,
        )
        for c in range(3)
    ]
    for copy in back:
        copy.start()

    ow_copy(0).start()
    hid_copy.start()
    og_copy.wait()
    dy_low = nt(up_o_ref[...], og[...]).astype(BF16)

    def project(block):
        ow_copy(block).wait()
        start = first_start if block < 2 else pair_start
        column = start + block % 2 * OW_BLOCK
        rows = slice(block * OW_BLOCK, (block + 1) * OW_BLOCK)
        through_adapter = tn(down_o_ref[:, lanes(column, OW_BLOCK)], dy_low)
        d_attn[rows, :] = (nt(ow[rows, :], og[...]) + 2.0 * through_adapter).astype(BF16)

    ow_copy(1).start()
    project(3)
    d_copy = remote(
        d_attn.at[HALF + AHEAD : HEADS_WIDTH, :],
        next_d,
        back_send_sem.at[3],
        back_recv_sem.at[3],
        previous,
    )
    d_copy.start()
    back.append(d_copy)
    for copy in qkv_copies[0]:
        copy.start()
    ow_copy(2).start()
    for copy in qkv_copies[1]:
        copy.start()

    hid_copy.wait()
    low_in = nt(down_ref[...], hid[...]).astype(BF16)
    thin[...] = jnp.concatenate([dy_low, low_in], axis=0)
    thin_copies = [
        remote(thin, next_thin, small_send_sem.at[0], small_recv_sem.at[0], previous),
        remote(
            thin.at[2 * RANK :], far_low, small_send_sem.at[1], small_recv_sem.at[1], following
        ),
    ]
    for copy in thin_copies:
        copy.start()
    project(0)
    project(1)
    project(2)

    key_row = lax.broadcasted_iota(jnp.int32, (TOKENS, TOKENS), 0)
    query_column = lax.broadcasted_iota(jnp.int32, (TOKENS, TOKENS), 1)
    seen = key_row <= query_column

    def head(q_head, d_head, keys, values):
        scores = [nt(key, q_head) * EXP2_SCALE for key in keys]
        scores[0] = jnp.where(seen, scores[0], -jnp.inf)
        row_max = functools.reduce(
            jnp.maximum, [jnp.max(score, axis=0, keepdims=True) for score in scores]
        )
        raised = [jnp.exp2(score - row_max) for score in scores]
        total = sum(jnp.sum(r, axis=0, keepdims=True) for r in raised)
        inverse = 1.0 / total
        probs = [r * inverse for r in raised]
        probs_low = [p.astype(BF16) for p in probs]
        d_probs = [nn(value, d_head) for value in values]
        row_dot = sum(
            jnp.sum(p * d, axis=0, keepdims=True) for p, d in zip(probs, d_probs)
        )
        d_scores = [(p * (d - row_dot)).astype(BF16) for p, d in zip(probs, d_probs)]
        attended = sum(tn(value, p) for value, p in zip(values, probs_low)).astype(BF16)
        d_query = (sum(tn(key, s) for key, s in zip(keys, d_scores)) * SCALE).astype(BF16)
        d_keys = [(nn(s, q_head) * SCALE).astype(BF16) for s in d_scores]
        d_values = [nt(p, d_head).astype(BF16) for p in probs_low]
        return attended, d_query, d_keys, d_values

    for copy in qkv_copies[0]:
        copy.wait()

    def first_heads(j, carry):
        for i in range(FIRST_STEP):
            at = (j * FIRST_STEP + i) * HEAD
            cols, rows = lanes(at, HEAD), pl.ds(pl.multiple_of(at, HEAD), HEAD)
            att[rows, :], dq[rows, :], d_keys, d_values = head(
                q[:, cols], d_attn[rows, :], [k[:, cols]], [v[:, cols]]
            )
            dk[:, cols], dv[:, cols] = d_keys[0], d_values[0]
        return carry

    lax.fori_loop(0, 8 // FIRST_STEP, first_heads, 0)

    first = lanes(first_start, HALF)
    totals[:RANK] = nn(up_ref[0, :, first], dq[:HALF, :])
    totals[RANK : 2 * RANK] = nt(up_ref[1, :, first], dk[:, :HALF])
    totals[2 * RANK : 3 * RANK] = nt(up_ref[2, :, first], dv[:, :HALF])
    totals[3 * RANK :] = nn(down_o_ref[:, first], att[:HALF, :])
    first_slot = LATE_SLOTS + first_start // TILE
    pair_slot = LATE_SLOTS + pair_start // TILE

    def pack(slot, ups, down_o):
        for n in range(down_o.shape[1] // TILE):
            low[slot + n] = stacked(tile_of(ups[0], n), tile_of(ups[1], n))
            low[SLOTS + slot + n] = stacked(tile_of(ups[2], n), tile_of(down_o, n))

    def ups_of(low_in_all, rows, cols, d_query, d_key, d_value):
        return [
            nt(low_in_all[:RANK], d_query[rows, :]),
            nn(low_in_all[RANK : 2 * RANK], d_key[:, cols]),
            nn(low_in_all[2 * RANK :], d_value[:, cols]),
        ]

    ahead = slice(0, AHEAD)
    pack(first_slot, ups_of(low_in, ahead, ahead, dq, dk, dv), nt(dy_low, att[:AHEAD, :]))
    for n in (6, 7):
        low[pair_slot + n] = jnp.zeros((16, TILE), BF16)
        low[SLOTS + pair_slot + n] = jnp.zeros((16, TILE), BF16)

    for copy in qkv_copies[1]:
        copy.wait()

    def arrived(ref, sem):
        pltpu.make_async_copy(ref, ref, sem).wait()

    whole = slice(0, BACK)
    turned = lanes(first_start + AHEAD, BACK)

    def next_device_heads():
        for c in range(3):
            arrived(next_qkv.at[c], back_recv_sem.at[c])
        arrived(next_d, back_recv_sem.at[3])
        arrived(next_thin, small_recv_sem.at[0])
        for i in range(2):
            part = slice(i * HEAD, (i + 1) * HEAD)
            cols = slice(AHEAD + i * HEAD, AHEAD + (i + 1) * HEAD)
            next_att[part, :], next_dq[part, :], d_keys, d_values = head(
                next_qkv[0, :, part],
                next_d[part, :],
                [next_qkv[1, :, part], k[:, cols]],
                [next_qkv[2, :, part], v[:, cols]],
            )
            next_dk[:, part], dk_cross[:, part] = d_keys
            next_dv[:, part], dv_cross[:, part] = d_values
        next_send[:RANK] = nn(up_ref[0, :, turned], next_dq[...])
        next_send[RANK : 2 * RANK] = nt(up_ref[1, :, turned], next_dk[...])
        next_send[2 * RANK : 3 * RANK] = nt(up_ref[2, :, turned], next_dv[...])
        next_send[3 * RANK :] = nn(down_o_ref[:, turned], next_att[...])
        next_copy.start()
        totals[RANK : 2 * RANK] += nt(up_ref[1, :, turned], dk_cross[...])
        totals[2 * RANK : 3 * RANK] += nt(up_ref[2, :, turned], dv_cross[...])
        own = ups_of(
            low_in, slice(AHEAD, HALF), slice(AHEAD, HALF), dq, dk, dv
        )
        other = ups_of(next_thin[RANK:], whole, whole, next_dq, next_dk, next_dv)
        ups = [a + b for a, b in zip(own, other)]
        ups[1] += nn(low_in[RANK : 2 * RANK], dk_cross[...])
        ups[2] += nn(low_in[2 * RANK :], dv_cross[...])
        down_o = nt(dy_low, att[AHEAD:HALF, :]) + nt(next_thin[:RANK], next_att[...])
        pack(first_slot + 6, ups, down_o)

    next_copy = remote(
        next_send, next_recv, small_send_sem.at[3], small_recv_sem.at[3], following
    )

    def pair_heads(j, carry):
        @pl.when(j == 2)
        def _():
            next_device_heads()

        for c, ref in ((0, far_k), (1, far_v)):
            arrived(ref.at[:, lanes(j * 256, 256)], kv_recv_sem.at[j, c])
        for i in range(2):
            far_cols = lanes(j * 256 + i * HEAD, HEAD)
            at = HALF + j * 256 + i * HEAD
            cols, rows = lanes(at, HEAD), pl.ds(pl.multiple_of(at, HEAD), HEAD)
            att[rows, :], dq[rows, :], d_keys, d_values = head(
                q[:, cols],
                d_attn[rows, :],
                [k[:, cols], far_k[:, far_cols]],
                [v[:, cols], far_v[:, far_cols]],
            )
            dk[:, cols], dk_far[:, far_cols] = d_keys
            dv[:, cols], dv_far[:, far_cols] = d_values
        return carry

    lax.fori_loop(0, 3, pair_heads, 0)

    pair = lanes(pair_start, AHEAD)
    far_send[:RANK] = nt(up_ref[1, :, pair], dk_far[...])
    far_send[RANK:] = nt(up_ref[2, :, pair], dv_far[...])
    far_copy = remote(far_send, far_recv, small_send_sem.at[2], small_recv_sem.at[2], previous)
    far_copy.start()

    z_place = [lax.rem(ctx + 2 + n, 4) for n in range(4)]
    x_place = lax.rem(ctx // 4, 4)
    y_place = ctx // 16

    other_core = (y_lo * 2 + 1 - core, ctx)
    chip = ctx * 2 + y_lo
    mine = core * SLOTS
    theirs = (1 - core) * SLOTS

    def to_sibling(start, count, n):
        return remote(
            low.at[pl.ds(theirs + start, count)],
            sibling.at[start : start + count],
            sibling_sems.at[n, 0],
            sibling_sems.at[n, 1],
            other_core,
        )

    def add_sibling(start, count):
        def add(n, carry):
            at = start + n
            low[mine + at] = (low[mine + at].astype(F32) + sibling[at].astype(F32)).astype(BF16)
            return carry

        lax.fori_loop(0, count, add, 0, unroll=8)

    def send_tiles(count, late):
        y_of = [lax.rem(z + core + (0 if late else 1), 2) for z in z_place]

        def send(j, carry):
            line = lax.rem(x_place + 2 + j, 4) * 4
            if count == 32:
                line += lax.rem(y_place + 1 + j // 4, 2) * 16
            for z, to_y in zip(z_place, y_of):
                to = line + z

                @pl.when(jnp.logical_or(to != ctx, to_y != y_lo))
                def _():
                    remote(
                        low.at[mine + to + (0 if late else LATE_SLOTS)],
                        parts.at[chip],
                        part_send_sem,
                        part_recv_sem,
                        (to_y * 2 + core, to),
                    ).start()

            return carry

        lax.fori_loop(0, count // 4, send, 0)

    pair_rows = slice(HALF, HALF + AHEAD)
    arrived(next_recv, small_recv_sem.at[3])
    low_o = (
        totals[3 * RANK :]
        + next_recv[3 * RANK :]
        + nn(down_o_ref[:, pair], att[pair_rows, :])
    ).astype(BF16)
    up_o = nn(low_o, og[...])
    for n in range(16):
        low[SLOTS + 16 + n] = stacked(tile_of(up_o, n), tile_of(up_o, n + 16))

    arrived(far_low, small_recv_sem.at[1])
    ups = ups_of(low_in, pair_rows, pair_rows, dq, dk, dv)
    ups[1] += nn(far_low[:RANK], dk_far[...])
    ups[2] += nn(far_low[RANK:], dv_far[...])
    pack(pair_slot, ups, nt(dy_low, att[pair_rows, :]))
    early_copy = to_sibling(LATE_SLOTS, 16, 0)
    early_copy.start()

    d_low = totals[: 3 * RANK] + next_recv[: 3 * RANK]
    d_low += jnp.concatenate(
        [
            nn(up_ref[0, :, pair], dq[pair_rows, :]),
            nt(up_ref[1, :, pair], dk[:, pair_rows]),
            nt(up_ref[2, :, pair], dv[:, pair_rows]),
        ],
        axis=0,
    )
    arrived(far_recv, small_recv_sem.at[2])
    d_low += jnp.concatenate([jnp.zeros((RANK, TOKENS), F32), far_recv[...]], axis=0)
    d_low = d_low.astype(BF16)
    d_low_ref[...] = d_low
    down = nn(d_low, hid[...])
    third = down[2 * RANK :]
    for n in range(32):
        low[n] = tile_of(down[: 2 * RANK], n).astype(BF16)
    for n in range(16):
        low[SLOTS + n] = stacked(tile_of(third, n), tile_of(third, n + 16))
    late_copy = to_sibling(0, LATE_SLOTS, 1)
    late_copy.start()
    arrived(sibling.at[LATE_SLOTS:SLOTS], sibling_sems.at[0, 1])
    add_sibling(LATE_SLOTS, 16)
    arrived(sibling.at[0:LATE_SLOTS], sibling_sems.at[1, 1])
    add_sibling(0, LATE_SLOTS)
    send_tiles(32, True)
    send_tiles(16, False)

    is_late = lax.rem(ctx + core, 2) == y_lo
    is_owner = jnp.logical_or(is_late, ctx < 16)
    slot = jnp.where(is_late, ctx, LATE_SLOTS + ctx)

    @pl.when(is_owner)
    def _():
        parts[chip] = low[mine + slot]
        arrived(parts.at[0 : CHIPS - 1], part_recv_sem)

        def add(n, total):
            return total + parts[n].astype(F32)

        total = lax.fori_loop(0, CHIPS, add, jnp.zeros((16, TILE), F32), unroll=8)
        summed_ref[core, slot] = (total * GRAD_SCALE).astype(BF16)

        def spread(j, carry):
            line = lax.rem(x_place + 2 + j, 4) * 4 + lax.rem(y_place + 1 + j // 4 % 2, 2) * 16
            to_y = lax.rem(y_lo + 1 + j // 8, 2)
            for z in z_place:
                to = line + z

                @pl.when(jnp.logical_or(to != ctx, to_y != y_lo))
                def _():
                    remote(
                        summed_ref.at[core, slot],
                        summed_ref.at[core, slot],
                        sum_send_sem,
                        sum_recv_sem,
                        (to_y * 2 + core, to),
                    ).start()

            return carry

        lax.fori_loop(0, 16, spread, 0)
        arrived(parts.at[0 : SLOTS - 1], sum_recv_sem)

    @pl.when(jnp.logical_not(is_owner))
    def _():
        arrived(parts.at[0:SLOTS], sum_recv_sem)

    last = remote(
        summed_ref.at[core],
        summed_ref.at[core],
        last_sems.at[0],
        last_sems.at[1],
        other_core,
    )
    last.start()

    @pl.when(is_owner)
    def _():
        arrived(low.at[0 : SLOTS - 1], part_send_sem)
        arrived(low.at[0:63], sum_send_sem)

    @pl.when(jnp.logical_not(is_owner))
    def _():
        arrived(low.at[0:SLOTS], part_send_sem)

    for copy in sent + back + thin_copies + [far_copy, next_copy, early_copy, late_copy]:
        copy.wait_send()
    last.wait()


def attention_part(hidden, projected, gradient, weight, down, up, down_o, up_o):
    ahead = VMEM((TOKENS, AHEAD), BF16)
    square = VMEM((TOKENS, BACK), BF16)
    whole = VMEM((TOKENS, HEADS_WIDTH), BF16)
    flipped = VMEM((HEADS_WIDTH, TOKENS), BF16)
    wide = VMEM((TOKENS, MODEL), BF16)
    anywhere = pl.BlockSpec(memory_space=pl.ANY)
    resident = pl.BlockSpec(memory_space=VMEM)
    return pl.pallas_call(
        attention_kernel,
        out_shape=(
            jax.ShapeDtypeStruct((3 * RANK, TOKENS), BF16),
            jax.ShapeDtypeStruct((2, SLOTS, 16, TILE), BF16),
        ),
        in_specs=[anywhere] * 4 + [resident] * 4,
        out_specs=(resident, resident),
        scratch_shapes=[
            wide,
            whole,
            whole,
            whole,
            wide,
            VMEM((HEADS_WIDTH, MODEL), BF16),
            ahead,
            ahead,
            VMEM((3, TOKENS, BACK), BF16),
            square,
            flipped,
            flipped,
            flipped,
            whole,
            whole,
            ahead,
            ahead,
            square,
            square,
            square,
            square,
            square,
            square,
            VMEM((4 * RANK, TOKENS), BF16),
            VMEM((2 * RANK, TOKENS), BF16),
            VMEM((4 * RANK, TOKENS), BF16),
            VMEM((4 * RANK, TOKENS), F32),
            VMEM((2 * RANK, TOKENS), F32),
            VMEM((2 * RANK, TOKENS), F32),
            VMEM((4 * RANK, TOKENS), F32),
            VMEM((4 * RANK, TOKENS), F32),
            VMEM((2 * SLOTS, 16, TILE), BF16),
            VMEM((CHIPS, 16, TILE), BF16),
            DMA((2,)),
            DMA((4,)),
            DMA((2, 3)),
            DMA((3, 2)),
            DMA((3, 2)),
            DMA((4,)),
            DMA((4,)),
            DMA((4,)),
            DMA((4,)),
            DMA,
            DMA,
            DMA,
            DMA,
            DMA((2,)),
            VMEM((SLOTS, 16, TILE), BF16),
            DMA((2, 2)),
        ],
        compiler_params=pltpu.CompilerParams(
            collective_id=0, has_side_effects=True, vmem_limit_bytes=56 << 20
        ),
    )(hidden, projected, gradient, weight, down, up, down_o, up_o)


def finish_kernel(
    summed_hbm,
    d_low_hbm,
    down_hbm,
    input_hbm,
    grad_down_ref,
    grad_up_ref,
    down_o_ref,
    up_o_ref,
    summed,
    d_low,
    down,
    result,
    in_sems,
    sems,
):
    fetches = [
        pltpu.make_async_copy(source, target, in_sems.at[n])
        for n, (source, target) in enumerate(
            ((d_low_hbm, d_low), (down_hbm, down), (summed_hbm, summed))
        )
    ]
    for fetch in fetches:
        fetch.start()
    fetches[0].wait()
    fetches[1].wait()
    copies = []
    for n in range(4):
        rows = slice(n * 64, (n + 1) * 64)
        result[rows, :] = (2.0 * tn(d_low[:, rows], down[...])).astype(BF16)
        copy = pltpu.make_async_copy(result.at[rows, :], input_hbm.at[0, rows, :], sems.at[n])
        copy.start()
        copies.append(copy)
    fetches[2].wait()

    def halves_of(kind, slot):
        tile = summed[kind, slot].astype(F32)
        return tile[:RANK].astype(BF16), tile[RANK:].astype(BF16)

    for n in range(32):
        cols = slice(n * TILE, (n + 1) * TILE)
        grad_down_ref[0, :, cols], grad_down_ref[1, :, cols] = halves_of(0, n)
    for n in range(16):
        cols = slice(n * TILE, (n + 1) * TILE)
        later = slice(HEADS_WIDTH + n * TILE, HEADS_WIDTH + (n + 1) * TILE)
        grad_down_ref[2, :, cols], grad_down_ref[2, :, later] = halves_of(1, n)
        up_o_ref[:, cols], up_o_ref[:, later] = halves_of(1, 16 + n)
        grad_up_ref[0, :, cols], grad_up_ref[1, :, cols] = halves_of(0, LATE_SLOTS + n)
        grad_up_ref[2, :, cols], down_o_ref[:, cols] = halves_of(1, LATE_SLOTS + n)
    for copy in copies:
        copy.wait()


def finish_part(summed, d_low, down):
    resident = pl.BlockSpec(memory_space=VMEM)
    anywhere = pl.BlockSpec(memory_space=pl.ANY)
    return pl.pallas_call(
        finish_kernel,
        out_shape=(
            jax.ShapeDtypeStruct((1, TOKENS, MODEL), BF16),
            jax.ShapeDtypeStruct((3, RANK, MODEL), BF16),
            jax.ShapeDtypeStruct((3, RANK, HEADS_WIDTH), BF16),
            jax.ShapeDtypeStruct((RANK, HEADS_WIDTH), BF16),
            jax.ShapeDtypeStruct((RANK, MODEL), BF16),
        ),
        in_specs=[anywhere] * 3,
        out_specs=(anywhere,) + (resident,) * 4,
        scratch_shapes=[
            VMEM((2, SLOTS, 16, TILE), BF16),
            VMEM((3 * RANK, TOKENS), BF16),
            VMEM((3 * RANK, MODEL), BF16),
            VMEM((TOKENS, MODEL), BF16),
            DMA((3,)),
            DMA((4,)),
        ],
        compiler_params=pltpu.CompilerParams(vmem_limit_bytes=60 << 20),
    )(summed, d_low, down)


def per_device(hidden, projected, gradient, weight, down, up, down_o, up_o):
    down = down.reshape(3 * RANK, MODEL)
    d_low, summed = attention_part(hidden, projected, gradient, weight, down, up, down_o, up_o)
    return finish_part(summed, d_low, down)


def solution(mesh):
    in_specs = (
        P("dp", "ctx", None),
        P(None, "dp", "ctx", None),
        P("dp", "ctx", None),
        P(),
        P(),
        P(),
        P(),
        P(),
    )
    out_specs = (P("dp", "ctx", None), P(), P(), P(), P())
    return jax.shard_map(
        per_device, mesh=mesh, in_specs=in_specs, out_specs=out_specs, check_vma=False
    )
```

```python
import functools
import math

import jax
import jax.numpy as jnp
from jax import lax
from jax.experimental import pallas as pl
from jax.experimental.pallas import tpu as pltpu
from jax.sharding import PartitionSpec as P

MESH = pl.DeviceIdType.MESH
DMA = pltpu.SemaphoreType.DMA
VMEM = pltpu.VMEM
F32 = jnp.float32
BF16 = jnp.bfloat16

TOKENS = 256
MODEL = 4096
HEADS_WIDTH = 2048
HALF = 1024
HEAD = 128
RANK = 8
CTX = 32
SCALE = 1.0 / math.sqrt(HEAD)
EXP2_SCALE = SCALE * math.log2(math.e)
GRAD_SCALE = 2.0 / 32768
OW_BLOCK = 512

TILE = 128
LATE_SLOTS = 32
SLOTS = 48
AHEAD = 768
BACK = 256
FIRST_STEP = 2
DEVICES = 128
CHIPS = 64


def nn(a, b):
    return lax.dot_general(a, b, (((1,), (0,)), ((), ())), preferred_element_type=F32)


def nt(a, b):
    return lax.dot_general(a, b, (((1,), (1,)), ((), ())), preferred_element_type=F32)


def tn(a, b):
    return lax.dot_general(a, b, (((0,), (0,)), ((), ())), preferred_element_type=F32)


def lanes(start, size):
    return pl.ds(pl.multiple_of(start, 128), size)


def stacked(top, bottom):
    return jnp.concatenate([top, bottom], axis=0).astype(BF16)


def tile_of(value, n):
    return value[:, n * TILE : (n + 1) * TILE]


def attention_kernel(
    hidden_hbm,
    projected_hbm,
    gradient_hbm,
    weight_hbm,
    down_ref,
    up_ref,
    down_o_ref,
    up_o_ref,
    result_hbm,
    summed_ref,
    hid,
    q,
    k,
    v,
    og,
    ow,
    far_k,
    far_v,
    next_qkv,
    next_d,
    d_attn,
    att,
    dq,
    dk,
    dv,
    dk_far,
    dv_far,
    next_att,
    next_dq,
    next_dk,
    next_dv,
    dk_cross,
    dv_cross,
    thin,
    far_low,
    next_thin,
    totals,
    far_send,
    far_recv,
    next_send,
    next_recv,
    low,
    parts,
    in_sem,
    ow_sem,
    qkv_sem,
    kv_send_sem,
    kv_recv_sem,
    back_send_sem,
    back_recv_sem,
    small_send_sem,
    small_recv_sem,
    part_send_sem,
    part_recv_sem,
    sum_send_sem,
    sum_recv_sem,
    last_sems,
    sibling,
    sibling_sems,
    result,
    result_sems,
):
    dp = lax.axis_index("dp")
    ctx = lax.axis_index("ctx")
    following = (dp, lax.rem(ctx + 1, CTX))
    previous = (dp, lax.rem(ctx + CTX - 1, CTX))
    parity = lax.rem(ctx, 2)
    first_start = parity * HALF
    pair_start = (1 - parity) * HALF
    core = lax.rem(dp, 2)
    y_lo = dp // 2
    me = dp * CTX + ctx

    def remote(source, target, send_sem, recv_sem, device):
        return pltpu.make_async_remote_copy(
            src_ref=source,
            dst_ref=target,
            send_sem=send_sem,
            recv_sem=recv_sem,
            device_id=device,
            device_id_type=MESH,
        )

    def ow_copy(block):
        start = first_start if block < 2 else pair_start
        row = start + block % 2 * OW_BLOCK
        return pltpu.make_async_copy(
            weight_hbm.at[pl.ds(pl.multiple_of(row, OW_BLOCK), OW_BLOCK), :],
            ow.at[block * OW_BLOCK : (block + 1) * OW_BLOCK, :],
            ow_sem.at[block],
        )

    og_copy = pltpu.make_async_copy(gradient_hbm.at[0], og, in_sem.at[0])
    hid_copy = pltpu.make_async_copy(hidden_hbm.at[0], hid, in_sem.at[1])
    qkv_copies = [
        [
            pltpu.make_async_copy(
                projected_hbm.at[c, 0, :, lanes(start, HALF)],
                ref.at[:, at * HALF : (at + 1) * HALF],
                qkv_sem.at[at, c],
            )
            for c, ref in enumerate((q, k, v))
        ]
        for at, start in enumerate((first_start, pair_start))
    ]
    og_copy.start()
    ow_copy(3).start()

    barrier = pltpu.get_barrier_semaphore()

    def greet(n, carry):
        other = lax.rem(ctx + n, CTX)
        for other_dp in range(4):

            @pl.when(jnp.logical_or(n != 0, other_dp != dp))
            def _():
                pl.semaphore_signal(
                    barrier, inc=1, device_id=(other_dp, other), device_id_type=MESH
                )

        return carry

    lax.fori_loop(0, CTX, greet, 0)
    pl.semaphore_wait(barrier, DEVICES - 1)
    sent = []
    for j in range(3):
        for c, ref in ((0, far_k), (1, far_v)):
            copy = remote(
                projected_hbm.at[c + 1, 0, :, lanes(first_start + j * 256, 256)],
                ref.at[:, j * 256 : (j + 1) * 256],
                kv_send_sem.at[j, c],
                kv_recv_sem.at[j, c],
                following,
            )
            copy.start()
            sent.append(copy)
    back = [
        remote(
            projected_hbm.at[c, 0, :, lanes(pair_start + AHEAD, BACK)],
            next_qkv.at[c],
            back_send_sem.at[c],
            back_recv_sem.at[c],
            previous,
        )
        for c in range(3)
    ]
    for copy in back:
        copy.start()

    ow_copy(0).start()
    hid_copy.start()
    og_copy.wait()
    dy_low = nt(up_o_ref[...], og[...]).astype(BF16)

    def project(block):
        ow_copy(block).wait()
        start = first_start if block < 2 else pair_start
        column = start + block % 2 * OW_BLOCK
        rows = slice(block * OW_BLOCK, (block + 1) * OW_BLOCK)
        through_adapter = tn(down_o_ref[:, lanes(column, OW_BLOCK)], dy_low)
        d_attn[rows, :] = (nt(ow[rows, :], og[...]) + 2.0 * through_adapter).astype(BF16)

    ow_copy(1).start()
    project(3)
    d_copy = remote(
        d_attn.at[HALF + AHEAD : HEADS_WIDTH, :],
        next_d,
        back_send_sem.at[3],
        back_recv_sem.at[3],
        previous,
    )
    d_copy.start()
    back.append(d_copy)
    for copy in qkv_copies[0]:
        copy.start()
    ow_copy(2).start()
    for copy in qkv_copies[1]:
        copy.start()

    hid_copy.wait()
    low_in = nt(down_ref[...], hid[...]).astype(BF16)
    thin[...] = jnp.concatenate([dy_low, low_in], axis=0)
    thin_copies = [
        remote(thin, next_thin, small_send_sem.at[0], small_recv_sem.at[0], previous),
        remote(
            thin.at[2 * RANK :], far_low, small_send_sem.at[1], small_recv_sem.at[1], following
        ),
    ]
    for copy in thin_copies:
        copy.start()
    project(0)
    project(1)
    project(2)

    key_row = lax.broadcasted_iota(jnp.int32, (TOKENS, TOKENS), 0)
    query_column = lax.broadcasted_iota(jnp.int32, (TOKENS, TOKENS), 1)
    seen = key_row <= query_column

    def head(q_head, d_head, keys, values):
        scores = [nt(key, q_head) * EXP2_SCALE for key in keys]
        scores[0] = jnp.where(seen, scores[0], -jnp.inf)
        row_max = functools.reduce(
            jnp.maximum, [jnp.max(score, axis=0, keepdims=True) for score in scores]
        )
        raised = [jnp.exp2(score - row_max) for score in scores]
        total = sum(jnp.sum(r, axis=0, keepdims=True) for r in raised)
        inverse = 1.0 / total
        probs = [r * inverse for r in raised]
        probs_low = [p.astype(BF16) for p in probs]
        d_probs = [nn(value, d_head) for value in values]
        row_dot = sum(
            jnp.sum(p * d, axis=0, keepdims=True) for p, d in zip(probs, d_probs)
        )
        d_scores = [(p * (d - row_dot)).astype(BF16) for p, d in zip(probs, d_probs)]
        attended = sum(tn(value, p) for value, p in zip(values, probs_low)).astype(BF16)
        d_query = (sum(tn(key, s) for key, s in zip(keys, d_scores)) * SCALE).astype(BF16)
        d_keys = [(nn(s, q_head) * SCALE).astype(BF16) for s in d_scores]
        d_values = [nt(p, d_head).astype(BF16) for p in probs_low]
        return attended, d_query, d_keys, d_values

    for copy in qkv_copies[0]:
        copy.wait()

    def first_heads(j, carry):
        for i in range(FIRST_STEP):
            at = (j * FIRST_STEP + i) * HEAD
            cols, rows = lanes(at, HEAD), pl.ds(pl.multiple_of(at, HEAD), HEAD)
            att[rows, :], dq[rows, :], d_keys, d_values = head(
                q[:, cols], d_attn[rows, :], [k[:, cols]], [v[:, cols]]
            )
            dk[:, cols], dv[:, cols] = d_keys[0], d_values[0]
        return carry

    lax.fori_loop(0, 8 // FIRST_STEP, first_heads, 0)

    first = lanes(first_start, HALF)
    totals[:RANK] = nn(up_ref[0, :, first], dq[:HALF, :])
    totals[RANK : 2 * RANK] = nt(up_ref[1, :, first], dk[:, :HALF])
    totals[2 * RANK : 3 * RANK] = nt(up_ref[2, :, first], dv[:, :HALF])
    totals[3 * RANK :] = nn(down_o_ref[:, first], att[:HALF, :])
    first_slot = LATE_SLOTS + first_start // TILE
    pair_slot = LATE_SLOTS + pair_start // TILE

    def pack(slot, ups, down_o):
        for n in range(down_o.shape[1] // TILE):
            low[slot + n] = stacked(tile_of(ups[0], n), tile_of(ups[1], n))
            low[SLOTS + slot + n] = stacked(tile_of(ups[2], n), tile_of(down_o, n))

    def ups_of(low_in_all, rows, cols, d_query, d_key, d_value):
        return [
            nt(low_in_all[:RANK], d_query[rows, :]),
            nn(low_in_all[RANK : 2 * RANK], d_key[:, cols]),
            nn(low_in_all[2 * RANK :], d_value[:, cols]),
        ]

    ahead = slice(0, AHEAD)
    pack(first_slot, ups_of(low_in, ahead, ahead, dq, dk, dv), nt(dy_low, att[:AHEAD, :]))
    for n in (6, 7):
        low[pair_slot + n] = jnp.zeros((16, TILE), BF16)
        low[SLOTS + pair_slot + n] = jnp.zeros((16, TILE), BF16)

    for copy in qkv_copies[1]:
        copy.wait()

    def arrived(ref, sem):
        pltpu.make_async_copy(ref, ref, sem).wait()

    whole = slice(0, BACK)
    turned = lanes(first_start + AHEAD, BACK)

    def next_device_heads():
        for c in range(3):
            arrived(next_qkv.at[c], back_recv_sem.at[c])
        arrived(next_d, back_recv_sem.at[3])
        arrived(next_thin, small_recv_sem.at[0])
        for i in range(2):
            part = slice(i * HEAD, (i + 1) * HEAD)
            cols = slice(AHEAD + i * HEAD, AHEAD + (i + 1) * HEAD)
            next_att[part, :], next_dq[part, :], d_keys, d_values = head(
                next_qkv[0, :, part],
                next_d[part, :],
                [next_qkv[1, :, part], k[:, cols]],
                [next_qkv[2, :, part], v[:, cols]],
            )
            next_dk[:, part], dk_cross[:, part] = d_keys
            next_dv[:, part], dv_cross[:, part] = d_values
        next_send[:RANK] = nn(up_ref[0, :, turned], next_dq[...])
        next_send[RANK : 2 * RANK] = nt(up_ref[1, :, turned], next_dk[...])
        next_send[2 * RANK : 3 * RANK] = nt(up_ref[2, :, turned], next_dv[...])
        next_send[3 * RANK :] = nn(down_o_ref[:, turned], next_att[...])
        next_copy.start()
        totals[RANK : 2 * RANK] += nt(up_ref[1, :, turned], dk_cross[...])
        totals[2 * RANK : 3 * RANK] += nt(up_ref[2, :, turned], dv_cross[...])
        own = ups_of(
            low_in, slice(AHEAD, HALF), slice(AHEAD, HALF), dq, dk, dv
        )
        other = ups_of(next_thin[RANK:], whole, whole, next_dq, next_dk, next_dv)
        ups = [a + b for a, b in zip(own, other)]
        ups[1] += nn(low_in[RANK : 2 * RANK], dk_cross[...])
        ups[2] += nn(low_in[2 * RANK :], dv_cross[...])
        down_o = nt(dy_low, att[AHEAD:HALF, :]) + nt(next_thin[:RANK], next_att[...])
        pack(first_slot + 6, ups, down_o)

    next_copy = remote(
        next_send, next_recv, small_send_sem.at[3], small_recv_sem.at[3], following
    )

    def pair_heads(j, carry):
        @pl.when(j == 2)
        def _():
            next_device_heads()

        for c, ref in ((0, far_k), (1, far_v)):
            arrived(ref.at[:, lanes(j * 256, 256)], kv_recv_sem.at[j, c])
        for i in range(2):
            far_cols = lanes(j * 256 + i * HEAD, HEAD)
            at = HALF + j * 256 + i * HEAD
            cols, rows = lanes(at, HEAD), pl.ds(pl.multiple_of(at, HEAD), HEAD)
            att[rows, :], dq[rows, :], d_keys, d_values = head(
                q[:, cols],
                d_attn[rows, :],
                [k[:, cols], far_k[:, far_cols]],
                [v[:, cols], far_v[:, far_cols]],
            )
            dk[:, cols], dk_far[:, far_cols] = d_keys
            dv[:, cols], dv_far[:, far_cols] = d_values
        return carry

    lax.fori_loop(0, 3, pair_heads, 0)

    pair = lanes(pair_start, AHEAD)
    far_send[:RANK] = nt(up_ref[1, :, pair], dk_far[...])
    far_send[RANK:] = nt(up_ref[2, :, pair], dv_far[...])
    far_copy = remote(far_send, far_recv, small_send_sem.at[2], small_recv_sem.at[2], previous)
    far_copy.start()

    z_place = [lax.rem(ctx + 2 + n, 4) for n in range(4)]
    x_place = lax.rem(ctx // 4, 4)
    y_place = ctx // 16

    other_core = (y_lo * 2 + 1 - core, ctx)
    chip = ctx * 2 + y_lo
    mine = core * SLOTS
    theirs = (1 - core) * SLOTS

    def to_sibling(start, count, n):
        return remote(
            low.at[pl.ds(theirs + start, count)],
            sibling.at[start : start + count],
            sibling_sems.at[n, 0],
            sibling_sems.at[n, 1],
            other_core,
        )

    def add_sibling(start, count):
        def add(n, carry):
            at = start + n
            low[mine + at] = (low[mine + at].astype(F32) + sibling[at].astype(F32)).astype(BF16)
            return carry

        lax.fori_loop(0, count, add, 0, unroll=8)

    def send_tiles(count, late):
        y_of = [lax.rem(z + core + (0 if late else 1), 2) for z in z_place]

        def send(j, carry):
            line = lax.rem(x_place + 2 + j, 4) * 4
            if count == 32:
                line += lax.rem(y_place + 1 + j // 4, 2) * 16
            for z, to_y in zip(z_place, y_of):
                to = line + z

                @pl.when(jnp.logical_or(to != ctx, to_y != y_lo))
                def _():
                    remote(
                        low.at[mine + to + (0 if late else LATE_SLOTS)],
                        parts.at[chip],
                        part_send_sem,
                        part_recv_sem,
                        (to_y * 2 + core, to),
                    ).start()

            return carry

        lax.fori_loop(0, count // 4, send, 0)

    pair_rows = slice(HALF, HALF + AHEAD)
    arrived(next_recv, small_recv_sem.at[3])
    low_o = (
        totals[3 * RANK :]
        + next_recv[3 * RANK :]
        + nn(down_o_ref[:, pair], att[pair_rows, :])
    ).astype(BF16)
    up_o = nn(low_o, og[...])
    for n in range(16):
        low[SLOTS + 16 + n] = stacked(tile_of(up_o, n), tile_of(up_o, n + 16))

    arrived(far_low, small_recv_sem.at[1])
    ups = ups_of(low_in, pair_rows, pair_rows, dq, dk, dv)
    ups[1] += nn(far_low[:RANK], dk_far[...])
    ups[2] += nn(far_low[RANK:], dv_far[...])
    pack(pair_slot, ups, nt(dy_low, att[pair_rows, :]))
    early_copy = to_sibling(LATE_SLOTS, 16, 0)
    early_copy.start()

    d_low = totals[: 3 * RANK] + next_recv[: 3 * RANK]
    d_low += jnp.concatenate(
        [
            nn(up_ref[0, :, pair], dq[pair_rows, :]),
            nt(up_ref[1, :, pair], dk[:, pair_rows]),
            nt(up_ref[2, :, pair], dv[:, pair_rows]),
        ],
        axis=0,
    )
    arrived(far_recv, small_recv_sem.at[2])
    d_low += jnp.concatenate([jnp.zeros((RANK, TOKENS), F32), far_recv[...]], axis=0)
    d_low = d_low.astype(BF16)
    down = nn(d_low, hid[...])
    third = down[2 * RANK :]
    for n in range(32):
        low[n] = tile_of(down[: 2 * RANK], n).astype(BF16)
    for n in range(16):
        low[SLOTS + n] = stacked(tile_of(third, n), tile_of(third, n + 16))
    late_copy = to_sibling(0, LATE_SLOTS, 1)
    late_copy.start()
    arrived(sibling.at[LATE_SLOTS:SLOTS], sibling_sems.at[0, 1])
    add_sibling(LATE_SLOTS, 16)
    arrived(sibling.at[0:LATE_SLOTS], sibling_sems.at[1, 1])
    add_sibling(0, LATE_SLOTS)
    send_tiles(32, True)
    send_tiles(16, False)

    result_copies = []
    for n in range(4):
        cols = slice(n * HALF, (n + 1) * HALF)
        result[:, cols] = (2.0 * tn(d_low, down_ref[:, cols])).astype(BF16)
        copy = pltpu.make_async_copy(result.at[:, cols], result_hbm.at[:, cols], result_sems.at[n])
        copy.start()
        result_copies.append(copy)

    is_late = lax.rem(ctx + core, 2) == y_lo
    is_owner = jnp.logical_or(is_late, ctx < 16)
    slot = jnp.where(is_late, ctx, LATE_SLOTS + ctx)

    @pl.when(is_owner)
    def _():
        parts[chip] = low[mine + slot]
        arrived(parts.at[0 : CHIPS - 1], part_recv_sem)

        def add(n, total):
            return total + parts[n].astype(F32)

        total = lax.fori_loop(0, CHIPS, add, jnp.zeros((16, TILE), F32), unroll=8)
        summed_ref[core, slot] = (total * GRAD_SCALE).astype(BF16)

        def spread(j, carry):
            line = lax.rem(x_place + 2 + j, 4) * 4 + lax.rem(y_place + 1 + j // 4 % 2, 2) * 16
            to_y = lax.rem(y_lo + 1 + j // 8, 2)
            for z in z_place:
                to = line + z

                @pl.when(jnp.logical_or(to != ctx, to_y != y_lo))
                def _():
                    remote(
                        summed_ref.at[core, slot],
                        summed_ref.at[core, slot],
                        sum_send_sem,
                        sum_recv_sem,
                        (to_y * 2 + core, to),
                    ).start()

            return carry

        lax.fori_loop(0, 16, spread, 0)
        arrived(parts.at[0 : SLOTS - 1], sum_recv_sem)

    @pl.when(jnp.logical_not(is_owner))
    def _():
        arrived(parts.at[0:SLOTS], sum_recv_sem)

    last = remote(
        summed_ref.at[core],
        summed_ref.at[core],
        last_sems.at[0],
        last_sems.at[1],
        other_core,
    )
    last.start()

    @pl.when(is_owner)
    def _():
        arrived(low.at[0 : SLOTS - 1], part_send_sem)
        arrived(low.at[0:63], sum_send_sem)

    @pl.when(jnp.logical_not(is_owner))
    def _():
        arrived(low.at[0:SLOTS], part_send_sem)

    for copy in sent + back + thin_copies + [far_copy, next_copy, early_copy, late_copy]:
        copy.wait_send()
    for copy in result_copies:
        copy.wait()
    last.wait()


def attention_part(hidden, projected, gradient, weight, down, up, down_o, up_o):
    ahead = VMEM((TOKENS, AHEAD), BF16)
    square = VMEM((TOKENS, BACK), BF16)
    whole = VMEM((TOKENS, HEADS_WIDTH), BF16)
    flipped = VMEM((HEADS_WIDTH, TOKENS), BF16)
    wide = VMEM((TOKENS, MODEL), BF16)
    anywhere = pl.BlockSpec(memory_space=pl.ANY)
    resident = pl.BlockSpec(memory_space=VMEM)
    return pl.pallas_call(
        attention_kernel,
        out_shape=(
            jax.ShapeDtypeStruct((TOKENS, MODEL), BF16),
            jax.ShapeDtypeStruct((2, SLOTS, 16, TILE), BF16),
        ),
        in_specs=[anywhere] * 4 + [resident] * 4,
        out_specs=(anywhere, resident),
        scratch_shapes=[
            wide,
            whole,
            whole,
            whole,
            wide,
            VMEM((HEADS_WIDTH, MODEL), BF16),
            ahead,
            ahead,
            VMEM((3, TOKENS, BACK), BF16),
            square,
            flipped,
            flipped,
            flipped,
            whole,
            whole,
            ahead,
            ahead,
            square,
            square,
            square,
            square,
            square,
            square,
            VMEM((4 * RANK, TOKENS), BF16),
            VMEM((2 * RANK, TOKENS), BF16),
            VMEM((4 * RANK, TOKENS), BF16),
            VMEM((4 * RANK, TOKENS), F32),
            VMEM((2 * RANK, TOKENS), F32),
            VMEM((2 * RANK, TOKENS), F32),
            VMEM((4 * RANK, TOKENS), F32),
            VMEM((4 * RANK, TOKENS), F32),
            VMEM((2 * SLOTS, 16, TILE), BF16),
            VMEM((CHIPS, 16, TILE), BF16),
            DMA((2,)),
            DMA((4,)),
            DMA((2, 3)),
            DMA((3, 2)),
            DMA((3, 2)),
            DMA((4,)),
            DMA((4,)),
            DMA((4,)),
            DMA((4,)),
            DMA,
            DMA,
            DMA,
            DMA,
            DMA((2,)),
            VMEM((SLOTS, 16, TILE), BF16),
            DMA((2, 2)),
            wide,
            DMA((4,)),
        ],
        compiler_params=pltpu.CompilerParams(
            collective_id=0, has_side_effects=True, vmem_limit_bytes=56 << 20
        ),
    )(hidden, projected, gradient, weight, down, up, down_o, up_o)


def finish_kernel(
    summed_hbm,
    result_hbm,
    input_hbm,
    grad_down_hbm,
    grad_up_hbm,
    down_o_hbm,
    up_o_hbm,
    grad_down_ref,
    grad_up_ref,
    down_o_ref,
    up_o_ref,
    summed,
    result,
    fetch_sem,
    in_sems,
    sems,
    out_sems,
):
    fetch = pltpu.make_async_copy(summed_hbm, summed, fetch_sem)
    fetch.start()
    rows_of = [slice(n * 64, (n + 1) * 64) for n in range(4)]
    fetches = [
        pltpu.make_async_copy(result_hbm.at[rows, :], result.at[rows, :], in_sems.at[n])
        for n, rows in enumerate(rows_of)
    ]
    for copy in fetches:
        copy.start()
    fetch.wait()

    def halves_of(kind, slot):
        tile = summed[kind, slot].astype(F32)
        return tile[:RANK].astype(BF16), tile[RANK:].astype(BF16)

    copies = []

    def pass_on(n):
        fetches[n].wait()
        rows = rows_of[n]
        copy = pltpu.make_async_copy(result.at[rows, :], input_hbm.at[0, rows, :], sems.at[n])
        copy.start()
        copies.append(copy)

    def send_out(source, target, n):
        copy = pltpu.make_async_copy(source, target, out_sems.at[n])
        copy.start()
        copies.append(copy)

    for n in range(16):
        cols = slice(n * TILE, (n + 1) * TILE)
        later = slice(HEADS_WIDTH + n * TILE, HEADS_WIDTH + (n + 1) * TILE)
        grad_down_ref[0, :, cols], grad_down_ref[1, :, cols] = halves_of(0, n)
        grad_down_ref[0, :, later], grad_down_ref[1, :, later] = halves_of(0, 16 + n)
        grad_down_ref[2, :, cols], grad_down_ref[2, :, later] = halves_of(1, n)
    send_out(grad_down_ref, grad_down_hbm, 0)
    pass_on(0)
    pass_on(1)
    for n in range(16):
        cols = slice(n * TILE, (n + 1) * TILE)
        later = slice(HEADS_WIDTH + n * TILE, HEADS_WIDTH + (n + 1) * TILE)
        up_o_ref[:, cols], up_o_ref[:, later] = halves_of(1, 16 + n)
        grad_up_ref[0, :, cols], grad_up_ref[1, :, cols] = halves_of(0, LATE_SLOTS + n)
        grad_up_ref[2, :, cols], down_o_ref[:, cols] = halves_of(1, LATE_SLOTS + n)
    send_out(grad_up_ref, grad_up_hbm, 1)
    send_out(down_o_ref, down_o_hbm, 2)
    send_out(up_o_ref, up_o_hbm, 3)
    pass_on(2)
    pass_on(3)
    for copy in copies:
        copy.wait()


def finish_part(summed, result):
    anywhere = pl.BlockSpec(memory_space=pl.ANY)
    return pl.pallas_call(
        finish_kernel,
        out_shape=(
            jax.ShapeDtypeStruct((1, TOKENS, MODEL), BF16),
            jax.ShapeDtypeStruct((3, RANK, MODEL), BF16),
            jax.ShapeDtypeStruct((3, RANK, HEADS_WIDTH), BF16),
            jax.ShapeDtypeStruct((RANK, HEADS_WIDTH), BF16),
            jax.ShapeDtypeStruct((RANK, MODEL), BF16),
        ),
        in_specs=[anywhere] * 2,
        out_specs=(anywhere,) * 5,
        scratch_shapes=[
            VMEM((3, RANK, MODEL), BF16),
            VMEM((3, RANK, HEADS_WIDTH), BF16),
            VMEM((RANK, HEADS_WIDTH), BF16),
            VMEM((RANK, MODEL), BF16),
            VMEM((2, SLOTS, 16, TILE), BF16),
            VMEM((TOKENS, MODEL), BF16),
            DMA,
            DMA((4,)),
            DMA((4,)),
            DMA((4,)),
        ],
        compiler_params=pltpu.CompilerParams(vmem_limit_bytes=60 << 20),
    )(summed, result)


def per_device(hidden, projected, gradient, weight, down, up, down_o, up_o):
    down = down.reshape(3 * RANK, MODEL)
    result, summed = attention_part(hidden, projected, gradient, weight, down, up, down_o, up_o)
    return finish_part(summed, result)


def solution(mesh):
    in_specs = (
        P("dp", "ctx", None),
        P(None, "dp", "ctx", None),
        P("dp", "ctx", None),
        P(),
        P(),
        P(),
        P(),
        P(),
    )
    out_specs = (P("dp", "ctx", None), P(), P(), P(), P())
    return jax.shard_map(
        per_device, mesh=mesh, in_specs=in_specs, out_specs=out_specs, check_vma=False
    )
```

```python
import functools
import math

import jax
import jax.numpy as jnp
from jax import lax
from jax.experimental import pallas as pl
from jax.experimental.pallas import tpu as pltpu
from jax.sharding import PartitionSpec as P

MESH = pl.DeviceIdType.MESH
DMA = pltpu.SemaphoreType.DMA
VMEM = pltpu.VMEM
F32 = jnp.float32
BF16 = jnp.bfloat16

TOKENS = 256
MODEL = 4096
HEADS_WIDTH = 2048
HALF = 1024
HEAD = 128
RANK = 8
CTX = 32
SCALE = 1.0 / math.sqrt(HEAD)
EXP2_SCALE = SCALE * math.log2(math.e)
GRAD_SCALE = 2.0 / 32768
OW_BLOCK = 512

TILE = 128
LATE_SLOTS = 32
SLOTS = 48
AHEAD = 768
BACK = 256
FIRST_STEP = 4
DEVICES = 128
CHIPS = 64


def nn(a, b):
    return lax.dot_general(a, b, (((1,), (0,)), ((), ())), preferred_element_type=F32)


def nt(a, b):
    return lax.dot_general(a, b, (((1,), (1,)), ((), ())), preferred_element_type=F32)


def tn(a, b):
    return lax.dot_general(a, b, (((0,), (0,)), ((), ())), preferred_element_type=F32)


def lanes(start, size):
    return pl.ds(pl.multiple_of(start, 128), size)


def stacked(top, bottom):
    return jnp.concatenate([top, bottom], axis=0).astype(BF16)


def tile_of(value, n):
    return value[:, n * TILE : (n + 1) * TILE]


def attention_kernel(
    hidden_hbm,
    projected_hbm,
    gradient_hbm,
    weight_hbm,
    down_ref,
    up_ref,
    down_o_ref,
    up_o_ref,
    result_hbm,
    summed_ref,
    hid,
    q,
    k,
    v,
    og,
    ow,
    far_k,
    far_v,
    next_qkv,
    next_d,
    d_attn,
    att,
    dq,
    dk,
    dv,
    dk_far,
    dv_far,
    next_att,
    next_dq,
    next_dk,
    next_dv,
    dk_cross,
    dv_cross,
    thin,
    far_low,
    next_thin,
    totals,
    far_send,
    far_recv,
    next_send,
    next_recv,
    low,
    parts,
    in_sem,
    ow_sem,
    qkv_sem,
    kv_send_sem,
    kv_recv_sem,
    back_send_sem,
    back_recv_sem,
    small_send_sem,
    small_recv_sem,
    part_send_sem,
    part_recv_sem,
    sum_send_sem,
    sum_recv_sem,
    last_sems,
    sibling,
    sibling_sems,
    result,
    result_sems,
):
    dp = lax.axis_index("dp")
    ctx = lax.axis_index("ctx")
    following = (dp, lax.rem(ctx + 1, CTX))
    previous = (dp, lax.rem(ctx + CTX - 1, CTX))
    parity = lax.rem(ctx, 2)
    first_start = parity * HALF
    pair_start = (1 - parity) * HALF
    core = lax.rem(dp, 2)
    y_lo = dp // 2
    me = dp * CTX + ctx

    def remote(source, target, send_sem, recv_sem, device):
        return pltpu.make_async_remote_copy(
            src_ref=source,
            dst_ref=target,
            send_sem=send_sem,
            recv_sem=recv_sem,
            device_id=device,
            device_id_type=MESH,
        )

    def ow_copy(block):
        start = first_start if block < 2 else pair_start
        row = start + block % 2 * OW_BLOCK
        return pltpu.make_async_copy(
            weight_hbm.at[pl.ds(pl.multiple_of(row, OW_BLOCK), OW_BLOCK), :],
            ow.at[block * OW_BLOCK : (block + 1) * OW_BLOCK, :],
            ow_sem.at[block],
        )

    og_copy = pltpu.make_async_copy(gradient_hbm.at[0], og, in_sem.at[0])
    hid_copy = pltpu.make_async_copy(hidden_hbm.at[0], hid, in_sem.at[1])
    qkv_copies = [
        [
            pltpu.make_async_copy(
                projected_hbm.at[c, 0, :, lanes(start, HALF)],
                ref.at[:, at * HALF : (at + 1) * HALF],
                qkv_sem.at[at, c],
            )
            for c, ref in enumerate((q, k, v))
        ]
        for at, start in enumerate((first_start, pair_start))
    ]
    og_copy.start()
    ow_copy(3).start()

    barrier = pltpu.get_barrier_semaphore()

    def greet(n, carry):
        other = lax.rem(ctx + n, CTX)
        for other_dp in range(4):

            @pl.when(jnp.logical_or(n != 0, other_dp != dp))
            def _():
                pl.semaphore_signal(
                    barrier, inc=1, device_id=(other_dp, other), device_id_type=MESH
                )

        return carry

    lax.fori_loop(0, CTX, greet, 0)
    pl.semaphore_wait(barrier, DEVICES - 1)
    sent = []
    for j in range(3):
        for c, ref in ((0, far_k), (1, far_v)):
            copy = remote(
                projected_hbm.at[c + 1, 0, :, lanes(first_start + j * 256, 256)],
                ref.at[:, j * 256 : (j + 1) * 256],
                kv_send_sem.at[j, c],
                kv_recv_sem.at[j, c],
                following,
            )
            copy.start()
            sent.append(copy)
    back = [
        remote(
            projected_hbm.at[c, 0, :, lanes(pair_start + AHEAD, BACK)],
            next_qkv.at[c],
            back_send_sem.at[c],
            back_recv_sem.at[c],
            previous,
        )
        for c in range(3)
    ]
    for copy in back:
        copy.start()

    ow_copy(0).start()
    hid_copy.start()
    og_copy.wait()
    dy_low = nt(up_o_ref[...], og[...]).astype(BF16)

    def project(block):
        ow_copy(block).wait()
        start = first_start if block < 2 else pair_start
        column = start + block % 2 * OW_BLOCK
        rows = slice(block * OW_BLOCK, (block + 1) * OW_BLOCK)
        through_adapter = tn(down_o_ref[:, lanes(column, OW_BLOCK)], dy_low)
        d_attn[rows, :] = (nt(ow[rows, :], og[...]) + 2.0 * through_adapter).astype(BF16)

    ow_copy(1).start()
    project(3)
    d_copy = remote(
        d_attn.at[HALF + AHEAD : HEADS_WIDTH, :],
        next_d,
        back_send_sem.at[3],
        back_recv_sem.at[3],
        previous,
    )
    d_copy.start()
    back.append(d_copy)
    for copy in qkv_copies[0]:
        copy.start()
    ow_copy(2).start()
    for copy in qkv_copies[1]:
        copy.start()

    hid_copy.wait()
    low_in = nt(down_ref[...], hid[...]).astype(BF16)
    thin[...] = jnp.concatenate([dy_low, low_in], axis=0)
    thin_copies = [
        remote(thin, next_thin, small_send_sem.at[0], small_recv_sem.at[0], previous),
        remote(
            thin.at[2 * RANK :], far_low, small_send_sem.at[1], small_recv_sem.at[1], following
        ),
    ]
    for copy in thin_copies:
        copy.start()
    project(0)
    project(1)
    project(2)

    key_row = lax.broadcasted_iota(jnp.int32, (TOKENS, TOKENS), 0)
    query_column = lax.broadcasted_iota(jnp.int32, (TOKENS, TOKENS), 1)
    seen = key_row <= query_column

    def head(q_head, d_head, keys, values):
        scores = [nt(key, q_head) * EXP2_SCALE for key in keys]
        scores[0] = jnp.where(seen, scores[0], -jnp.inf)
        row_max = functools.reduce(
            jnp.maximum, [jnp.max(score, axis=0, keepdims=True) for score in scores]
        )
        raised = [jnp.exp2(score - row_max) for score in scores]
        total = sum(jnp.sum(r, axis=0, keepdims=True) for r in raised)
        inverse = 1.0 / total
        probs = [r * inverse for r in raised]
        probs_low = [p.astype(BF16) for p in probs]
        d_probs = [nn(value, d_head) for value in values]
        row_dot = sum(
            jnp.sum(p * d, axis=0, keepdims=True) for p, d in zip(probs, d_probs)
        )
        d_scores = [(p * (d - row_dot)).astype(BF16) for p, d in zip(probs, d_probs)]
        attended = sum(tn(value, p) for value, p in zip(values, probs_low)).astype(BF16)
        d_query = (sum(tn(key, s) for key, s in zip(keys, d_scores)) * SCALE).astype(BF16)
        d_keys = [(nn(s, q_head) * SCALE).astype(BF16) for s in d_scores]
        d_values = [nt(p, d_head).astype(BF16) for p in probs_low]
        return attended, d_query, d_keys, d_values

    for copy in qkv_copies[0]:
        copy.wait()

    def first_heads(j, carry):
        for i in range(FIRST_STEP):
            at = (j * FIRST_STEP + i) * HEAD
            cols, rows = lanes(at, HEAD), pl.ds(pl.multiple_of(at, HEAD), HEAD)
            att[rows, :], dq[rows, :], d_keys, d_values = head(
                q[:, cols], d_attn[rows, :], [k[:, cols]], [v[:, cols]]
            )
            dk[:, cols], dv[:, cols] = d_keys[0], d_values[0]
        return carry

    lax.fori_loop(0, 8 // FIRST_STEP, first_heads, 0)

    first = lanes(first_start, HALF)
    totals[:RANK] = nn(up_ref[0, :, first], dq[:HALF, :])
    totals[RANK : 2 * RANK] = nt(up_ref[1, :, first], dk[:, :HALF])
    totals[2 * RANK : 3 * RANK] = nt(up_ref[2, :, first], dv[:, :HALF])
    totals[3 * RANK :] = nn(down_o_ref[:, first], att[:HALF, :])
    first_slot = LATE_SLOTS + first_start // TILE
    pair_slot = LATE_SLOTS + pair_start // TILE

    def pack(slot, ups, down_o):
        for n in range(down_o.shape[1] // TILE):
            low[slot + n] = stacked(tile_of(ups[0], n), tile_of(ups[1], n))
            low[SLOTS + slot + n] = stacked(tile_of(ups[2], n), tile_of(down_o, n))

    def ups_of(low_in_all, rows, cols, d_query, d_key, d_value):
        return [
            nt(low_in_all[:RANK], d_query[rows, :]),
            nn(low_in_all[RANK : 2 * RANK], d_key[:, cols]),
            nn(low_in_all[2 * RANK :], d_value[:, cols]),
        ]

    ahead = slice(0, AHEAD)
    pack(first_slot, ups_of(low_in, ahead, ahead, dq, dk, dv), nt(dy_low, att[:AHEAD, :]))
    for n in (6, 7):
        low[pair_slot + n] = jnp.zeros((16, TILE), BF16)
        low[SLOTS + pair_slot + n] = jnp.zeros((16, TILE), BF16)

    for copy in qkv_copies[1]:
        copy.wait()

    def arrived(ref, sem):
        pltpu.make_async_copy(ref, ref, sem).wait()

    whole = slice(0, BACK)
    turned = lanes(first_start + AHEAD, BACK)

    def next_device_heads():
        for c in range(3):
            arrived(next_qkv.at[c], back_recv_sem.at[c])
        arrived(next_d, back_recv_sem.at[3])
        arrived(next_thin, small_recv_sem.at[0])
        for i in range(2):
            part = slice(i * HEAD, (i + 1) * HEAD)
            cols = slice(AHEAD + i * HEAD, AHEAD + (i + 1) * HEAD)
            next_att[part, :], next_dq[part, :], d_keys, d_values = head(
                next_qkv[0, :, part],
                next_d[part, :],
                [next_qkv[1, :, part], k[:, cols]],
                [next_qkv[2, :, part], v[:, cols]],
            )
            next_dk[:, part], dk_cross[:, part] = d_keys
            next_dv[:, part], dv_cross[:, part] = d_values
        next_send[:RANK] = nn(up_ref[0, :, turned], next_dq[...])
        next_send[RANK : 2 * RANK] = nt(up_ref[1, :, turned], next_dk[...])
        next_send[2 * RANK : 3 * RANK] = nt(up_ref[2, :, turned], next_dv[...])
        next_send[3 * RANK :] = nn(down_o_ref[:, turned], next_att[...])
        next_copy.start()
        totals[RANK : 2 * RANK] += nt(up_ref[1, :, turned], dk_cross[...])
        totals[2 * RANK : 3 * RANK] += nt(up_ref[2, :, turned], dv_cross[...])
        own = ups_of(
            low_in, slice(AHEAD, HALF), slice(AHEAD, HALF), dq, dk, dv
        )
        other = ups_of(next_thin[RANK:], whole, whole, next_dq, next_dk, next_dv)
        ups = [a + b for a, b in zip(own, other)]
        ups[1] += nn(low_in[RANK : 2 * RANK], dk_cross[...])
        ups[2] += nn(low_in[2 * RANK :], dv_cross[...])
        down_o = nt(dy_low, att[AHEAD:HALF, :]) + nt(next_thin[:RANK], next_att[...])
        pack(first_slot + 6, ups, down_o)

    next_copy = remote(
        next_send, next_recv, small_send_sem.at[3], small_recv_sem.at[3], following
    )

    def pair_heads(j, carry):
        @pl.when(j == 2)
        def _():
            next_device_heads()

        for c, ref in ((0, far_k), (1, far_v)):
            arrived(ref.at[:, lanes(j * 256, 256)], kv_recv_sem.at[j, c])
        for i in range(2):
            far_cols = lanes(j * 256 + i * HEAD, HEAD)
            at = HALF + j * 256 + i * HEAD
            cols, rows = lanes(at, HEAD), pl.ds(pl.multiple_of(at, HEAD), HEAD)
            att[rows, :], dq[rows, :], d_keys, d_values = head(
                q[:, cols],
                d_attn[rows, :],
                [k[:, cols], far_k[:, far_cols]],
                [v[:, cols], far_v[:, far_cols]],
            )
            dk[:, cols], dk_far[:, far_cols] = d_keys
            dv[:, cols], dv_far[:, far_cols] = d_values
        return carry

    lax.fori_loop(0, 3, pair_heads, 0)

    pair = lanes(pair_start, AHEAD)
    far_send[:RANK] = nt(up_ref[1, :, pair], dk_far[...])
    far_send[RANK:] = nt(up_ref[2, :, pair], dv_far[...])
    far_copy = remote(far_send, far_recv, small_send_sem.at[2], small_recv_sem.at[2], previous)
    far_copy.start()

    z_place = [lax.rem(ctx + 2 + n, 4) for n in range(4)]
    x_place = lax.rem(ctx // 4, 4)
    y_place = ctx // 16

    other_core = (y_lo * 2 + 1 - core, ctx)
    chip = ctx * 2 + y_lo
    mine = core * SLOTS
    theirs = (1 - core) * SLOTS

    def to_sibling(start, count, n):
        return remote(
            low.at[pl.ds(theirs + start, count)],
            sibling.at[start : start + count],
            sibling_sems.at[n, 0],
            sibling_sems.at[n, 1],
            other_core,
        )

    def add_sibling(start, count):
        def add(n, carry):
            at = start + n
            low[mine + at] = (low[mine + at].astype(F32) + sibling[at].astype(F32)).astype(BF16)
            return carry

        lax.fori_loop(0, count, add, 0, unroll=8)

    def send_tiles(count, late):
        y_of = [lax.rem(z + core + (0 if late else 1), 2) for z in z_place]

        def send(j, carry):
            line = lax.rem(x_place + 2 + j, 4) * 4
            if count == 32:
                line += lax.rem(y_place + 1 + j // 4, 2) * 16
            for z, to_y in zip(z_place, y_of):
                to = line + z

                @pl.when(jnp.logical_or(to != ctx, to_y != y_lo))
                def _():
                    remote(
                        low.at[mine + to + (0 if late else LATE_SLOTS)],
                        parts.at[chip],
                        part_send_sem,
                        part_recv_sem,
                        (to_y * 2 + core, to),
                    ).start()

            return carry

        lax.fori_loop(0, count // 4, send, 0)

    pair_rows = slice(HALF, HALF + AHEAD)
    arrived(next_recv, small_recv_sem.at[3])
    low_o = (
        totals[3 * RANK :]
        + next_recv[3 * RANK :]
        + nn(down_o_ref[:, pair], att[pair_rows, :])
    ).astype(BF16)
    up_o = nn(low_o, og[...])
    for n in range(16):
        low[SLOTS + 16 + n] = stacked(tile_of(up_o, n), tile_of(up_o, n + 16))

    arrived(far_low, small_recv_sem.at[1])
    ups = ups_of(low_in, pair_rows, pair_rows, dq, dk, dv)
    ups[1] += nn(far_low[:RANK], dk_far[...])
    ups[2] += nn(far_low[RANK:], dv_far[...])
    pack(pair_slot, ups, nt(dy_low, att[pair_rows, :]))
    early_copy = to_sibling(LATE_SLOTS, 16, 0)
    early_copy.start()

    d_low = totals[: 3 * RANK] + next_recv[: 3 * RANK]
    d_low += jnp.concatenate(
        [
            nn(up_ref[0, :, pair], dq[pair_rows, :]),
            nt(up_ref[1, :, pair], dk[:, pair_rows]),
            nt(up_ref[2, :, pair], dv[:, pair_rows]),
        ],
        axis=0,
    )
    arrived(far_recv, small_recv_sem.at[2])
    d_low += jnp.concatenate([jnp.zeros((RANK, TOKENS), F32), far_recv[...]], axis=0)
    d_low = d_low.astype(BF16)
    down = nn(d_low, hid[...])
    third = down[2 * RANK :]
    for n in range(32):
        low[n] = tile_of(down[: 2 * RANK], n).astype(BF16)
    for n in range(16):
        low[SLOTS + n] = stacked(tile_of(third, n), tile_of(third, n + 16))
    late_copy = to_sibling(0, LATE_SLOTS, 1)
    late_copy.start()
    arrived(sibling.at[LATE_SLOTS:SLOTS], sibling_sems.at[0, 1])
    add_sibling(LATE_SLOTS, 16)
    arrived(sibling.at[0:LATE_SLOTS], sibling_sems.at[1, 1])
    add_sibling(0, LATE_SLOTS)
    send_tiles(32, True)
    send_tiles(16, False)

    result_copies = []
    for n in range(4):
        cols = slice(n * HALF, (n + 1) * HALF)
        result[:, cols] = (2.0 * tn(d_low, down_ref[:, cols])).astype(BF16)
        copy = pltpu.make_async_copy(result.at[:, cols], result_hbm.at[:, cols], result_sems.at[n])
        copy.start()
        result_copies.append(copy)

    is_late = lax.rem(ctx + core, 2) == y_lo
    is_owner = jnp.logical_or(is_late, ctx < 16)
    slot = jnp.where(is_late, ctx, LATE_SLOTS + ctx)

    @pl.when(is_owner)
    def _():
        parts[chip] = low[mine + slot]
        arrived(parts.at[0 : CHIPS - 1], part_recv_sem)

        def add(n, total):
            return total + parts[n].astype(F32)

        total = lax.fori_loop(0, CHIPS, add, jnp.zeros((16, TILE), F32), unroll=8)
        summed_ref[core, slot] = (total * GRAD_SCALE).astype(BF16)

        def spread(j, carry):
            line = lax.rem(x_place + 2 + j, 4) * 4 + lax.rem(y_place + 1 + j // 4 % 2, 2) * 16
            to_y = lax.rem(y_lo + 1 + j // 8, 2)
            for z in z_place:
                to = line + z

                @pl.when(jnp.logical_or(to != ctx, to_y != y_lo))
                def _():
                    remote(
                        summed_ref.at[core, slot],
                        summed_ref.at[core, slot],
                        sum_send_sem,
                        sum_recv_sem,
                        (to_y * 2 + core, to),
                    ).start()

            return carry

        lax.fori_loop(0, 16, spread, 0)
        arrived(parts.at[0 : SLOTS - 1], sum_recv_sem)

    @pl.when(jnp.logical_not(is_owner))
    def _():
        arrived(parts.at[0:SLOTS], sum_recv_sem)

    last = remote(
        summed_ref.at[core],
        summed_ref.at[core],
        last_sems.at[0],
        last_sems.at[1],
        other_core,
    )
    last.start()

    @pl.when(is_owner)
    def _():
        arrived(low.at[0 : SLOTS - 1], part_send_sem)
        arrived(low.at[0:63], sum_send_sem)

    @pl.when(jnp.logical_not(is_owner))
    def _():
        arrived(low.at[0:SLOTS], part_send_sem)

    for copy in sent + back + thin_copies + [far_copy, next_copy, early_copy, late_copy]:
        copy.wait_send()
    for copy in result_copies:
        copy.wait()
    last.wait()


def attention_part(hidden, projected, gradient, weight, down, up, down_o, up_o):
    ahead = VMEM((TOKENS, AHEAD), BF16)
    square = VMEM((TOKENS, BACK), BF16)
    whole = VMEM((TOKENS, HEADS_WIDTH), BF16)
    flipped = VMEM((HEADS_WIDTH, TOKENS), BF16)
    wide = VMEM((TOKENS, MODEL), BF16)
    anywhere = pl.BlockSpec(memory_space=pl.ANY)
    resident = pl.BlockSpec(memory_space=VMEM)
    return pl.pallas_call(
        attention_kernel,
        out_shape=(
            jax.ShapeDtypeStruct((TOKENS, MODEL), BF16),
            jax.ShapeDtypeStruct((2, SLOTS, 16, TILE), BF16),
        ),
        in_specs=[anywhere] * 4 + [resident] * 4,
        out_specs=(anywhere, resident),
        scratch_shapes=[
            wide,
            whole,
            whole,
            whole,
            wide,
            VMEM((HEADS_WIDTH, MODEL), BF16),
            ahead,
            ahead,
            VMEM((3, TOKENS, BACK), BF16),
            square,
            flipped,
            flipped,
            flipped,
            whole,
            whole,
            ahead,
            ahead,
            square,
            square,
            square,
            square,
            square,
            square,
            VMEM((4 * RANK, TOKENS), BF16),
            VMEM((2 * RANK, TOKENS), BF16),
            VMEM((4 * RANK, TOKENS), BF16),
            VMEM((4 * RANK, TOKENS), F32),
            VMEM((2 * RANK, TOKENS), F32),
            VMEM((2 * RANK, TOKENS), F32),
            VMEM((4 * RANK, TOKENS), F32),
            VMEM((4 * RANK, TOKENS), F32),
            VMEM((2 * SLOTS, 16, TILE), BF16),
            VMEM((CHIPS, 16, TILE), BF16),
            DMA((2,)),
            DMA((4,)),
            DMA((2, 3)),
            DMA((3, 2)),
            DMA((3, 2)),
            DMA((4,)),
            DMA((4,)),
            DMA((4,)),
            DMA((4,)),
            DMA,
            DMA,
            DMA,
            DMA,
            DMA((2,)),
            VMEM((SLOTS, 16, TILE), BF16),
            DMA((2, 2)),
            wide,
            DMA((4,)),
        ],
        compiler_params=pltpu.CompilerParams(
            collective_id=0, has_side_effects=True, vmem_limit_bytes=56 << 20
        ),
    )(hidden, projected, gradient, weight, down, up, down_o, up_o)


def finish_kernel(
    summed_hbm,
    result_hbm,
    input_hbm,
    grad_down_hbm,
    grad_up_hbm,
    down_o_hbm,
    up_o_hbm,
    grad_down_ref,
    grad_up_ref,
    down_o_ref,
    up_o_ref,
    summed,
    result,
    fetch_sem,
    in_sems,
    sems,
    out_sems,
):
    fetch = pltpu.make_async_copy(summed_hbm, summed, fetch_sem)
    fetch.start()
    rows_of = [slice(n * 64, (n + 1) * 64) for n in range(4)]
    fetches = [
        pltpu.make_async_copy(result_hbm.at[rows, :], result.at[rows, :], in_sems.at[n])
        for n, rows in enumerate(rows_of)
    ]
    for copy in fetches:
        copy.start()
    fetch.wait()

    def halves_of(kind, slot):
        tile = summed[kind, slot].astype(F32)
        return tile[:RANK].astype(BF16), tile[RANK:].astype(BF16)

    copies = []

    def pass_on(n):
        fetches[n].wait()
        rows = rows_of[n]
        copy = pltpu.make_async_copy(result.at[rows, :], input_hbm.at[0, rows, :], sems.at[n])
        copy.start()
        copies.append(copy)

    def send_out(source, target, n):
        copy = pltpu.make_async_copy(source, target, out_sems.at[n])
        copy.start()
        copies.append(copy)

    for n in range(16):
        cols = slice(n * TILE, (n + 1) * TILE)
        later = slice(HEADS_WIDTH + n * TILE, HEADS_WIDTH + (n + 1) * TILE)
        grad_down_ref[0, :, cols], grad_down_ref[1, :, cols] = halves_of(0, n)
        grad_down_ref[0, :, later], grad_down_ref[1, :, later] = halves_of(0, 16 + n)
        grad_down_ref[2, :, cols], grad_down_ref[2, :, later] = halves_of(1, n)
    send_out(grad_down_ref, grad_down_hbm, 0)
    pass_on(0)
    pass_on(1)
    for n in range(16):
        cols = slice(n * TILE, (n + 1) * TILE)
        later = slice(HEADS_WIDTH + n * TILE, HEADS_WIDTH + (n + 1) * TILE)
        up_o_ref[:, cols], up_o_ref[:, later] = halves_of(1, 16 + n)
        grad_up_ref[0, :, cols], grad_up_ref[1, :, cols] = halves_of(0, LATE_SLOTS + n)
        grad_up_ref[2, :, cols], down_o_ref[:, cols] = halves_of(1, LATE_SLOTS + n)
    send_out(grad_up_ref, grad_up_hbm, 1)
    send_out(down_o_ref, down_o_hbm, 2)
    send_out(up_o_ref, up_o_hbm, 3)
    pass_on(2)
    pass_on(3)
    for copy in copies:
        copy.wait()


def finish_part(summed, result):
    anywhere = pl.BlockSpec(memory_space=pl.ANY)
    return pl.pallas_call(
        finish_kernel,
        out_shape=(
            jax.ShapeDtypeStruct((1, TOKENS, MODEL), BF16),
            jax.ShapeDtypeStruct((3, RANK, MODEL), BF16),
            jax.ShapeDtypeStruct((3, RANK, HEADS_WIDTH), BF16),
            jax.ShapeDtypeStruct((RANK, HEADS_WIDTH), BF16),
            jax.ShapeDtypeStruct((RANK, MODEL), BF16),
        ),
        in_specs=[anywhere] * 2,
        out_specs=(anywhere,) * 5,
        scratch_shapes=[
            VMEM((3, RANK, MODEL), BF16),
            VMEM((3, RANK, HEADS_WIDTH), BF16),
            VMEM((RANK, HEADS_WIDTH), BF16),
            VMEM((RANK, MODEL), BF16),
            VMEM((2, SLOTS, 16, TILE), BF16),
            VMEM((TOKENS, MODEL), BF16),
            DMA,
            DMA((4,)),
            DMA((4,)),
            DMA((4,)),
        ],
        compiler_params=pltpu.CompilerParams(vmem_limit_bytes=60 << 20),
    )(summed, result)


def per_device(hidden, projected, gradient, weight, down, up, down_o, up_o):
    down = down.reshape(3 * RANK, MODEL)
    result, summed = attention_part(hidden, projected, gradient, weight, down, up, down_o, up_o)
    return finish_part(summed, result)


def solution(mesh):
    in_specs = (
        P("dp", "ctx", None),
        P(None, "dp", "ctx", None),
        P("dp", "ctx", None),
        P(),
        P(),
        P(),
        P(),
        P(),
    )
    out_specs = (P("dp", "ctx", None), P(), P(), P(), P())
    return jax.shard_map(
        per_device, mesh=mesh, in_specs=in_specs, out_specs=out_specs, check_vma=False
    )
```
